256 devices in a mesh: row: 8 (over z), col: 32 (over y, x, core).
Axes of the slice: x: 4, y: 4, z: 8, core: 2. Of those that a mesh axis runs over, the one named last changes fastest.
Arguments:
- source_latent: bfloat16 [64, 65536], P(None, ('row', 'col')), may hold values from -27 to 27
- target_latent: bfloat16 [64, 65536], P(None, 'col'), may hold values from -6 to 6
- log_source_mass: float32 [65536], P('row'), may hold values from -2 to 2
- log_target_mass: bfloat16 [65536], P('col'), may hold values from -2 to 2
- target_coords: bfloat16 [2, 65536], P(None, 'col'), may hold values from -2 to 2
- support: int32 [512, 32], P('row'), may hold values from 0 to 511, as said below
Outputs:
- source_potential: float32 [65536], P(('row', 'col'))
- target_potential: float32 [65536], P('col')
- projection: float32 [2, 65536], P(None, ('row', 'col'))
The draws below stay inside these ranges and needn't reach their ends.
Inputs may be any that keep to these rules, and one draw needn't show every extreme that they name: `support`: each source block lists 32 distinct target blocks. Of the 64 source blocks of one row shard, at most 192 listed entries fall into the 16 target blocks of one col shard, and exactly 192 for some col shard. Every target block is listed by some source block.
All inputs are finite; a program needn't handle non-finite values.
Results may differ from the reference program's by a relative error of at most 0.0003.
Values may be sent and summed in bfloat16 or wider, within the bound.
No kernel may reach another device: no remote copies, remote signals or barrier semaphores. Data moves between devices by JAX's collectives and lax.ppermute only.
A program may use at most 320 MiB of HBM per device.

```python
import jax
import jax.numpy as jnp
from jax import lax

LAT = 64
BLK = 128
ITERS = 2
SB = 64
TB = 16
KB = 32
NRB = 512
NTB = 512
NS = 65536
NT = 65536
N_ROW = 8
N_COL = 32


def target_values(key):
    normal_values = jax.random.normal(jax.random.fold_in(key, 101), (LAT, NTB * BLK), jnp.float32)
    return jnp.clip(normal_values, -6.0, 6.0)


def support_lists(key):
    seed_key = jax.random.fold_in(key, 202)
    per_device = KB // N_COL
    half_axis = N_COL // 2
    block_index = jnp.arange(NRB, dtype=jnp.int32)
    device_index = jnp.arange(N_COL, dtype=jnp.int32)[None, :]
    busy_table = jax.random.randint(jax.random.fold_in(seed_key, 1), (N_ROW,), 0, N_COL, dtype=jnp.int32)
    busy_device = busy_table[block_index // SB]
    is_busy = device_index == busy_device[:, None]
    protected = (device_index - block_index[:, None]) % N_COL < half_axis
    spare_count = jax.random.randint(jax.random.fold_in(seed_key, 2), (NRB, 1), 0, half_axis - 2, dtype=jnp.int32)
    far_value = jnp.int32(1 << 30)
    zero_keys = jax.random.randint(jax.random.fold_in(seed_key, 3), (NRB, N_COL), 0, 1 << 20, dtype=jnp.int32) * N_COL + device_index
    zero_keys = jnp.where(protected | is_busy, far_value, zero_keys)
    zero_rank = jnp.argsort(jnp.argsort(zero_keys, axis=1), axis=1)
    is_zero = zero_rank < spare_count + 2
    double_keys = jax.random.randint(jax.random.fold_in(seed_key, 4), (NRB, N_COL), 0, 1 << 20, dtype=jnp.int32) * N_COL + device_index
    double_keys = jnp.where(is_busy | is_zero, far_value, double_keys)
    double_rank = jnp.argsort(jnp.argsort(double_keys, axis=1), axis=1)
    is_double = double_rank < spare_count
    counts = jnp.where(is_busy, 3 * per_device, jnp.where(is_zero, 0, jnp.where(is_double, 2 * per_device, per_device)))
    offsets = jax.random.randint(jax.random.fold_in(seed_key, 5), (1, N_COL), 0, TB, dtype=jnp.int32)
    starts = (jnp.cumsum(counts, axis=0) - counts + offsets) % TB
    slot_index = jnp.arange(3 * per_device, dtype=jnp.int32)[None, None, :]
    block_ids = device_index[:, :, None] * TB + (starts[:, :, None] + slot_index) % TB
    live_slot = slot_index < counts[:, :, None]
    block_ids = block_ids.reshape(NRB, N_COL * 3 * per_device)
    live_slot = live_slot.reshape(NRB, N_COL * 3 * per_device)
    ordering = jnp.argsort(jnp.where(live_slot, 0, 1), axis=1, stable=True)
    return jnp.take_along_axis(block_ids, ordering, axis=1)[:, :KB].astype(jnp.int32)


def draw_support(key, part):
    listed = support_lists(key)
    return listed


def draw_target_latent(key, part):
    targets = target_values(key)
    return targets.astype(jnp.bfloat16)


def draw_source_latent(key, part):
    key = jax.random.fold_in(key, 3)
    values = jnp.clip(jax.random.normal(jax.random.fold_in(key, 1), (LAT, NRB * BLK), jnp.float32), -6.0, 6.0)
    return values.astype(jnp.bfloat16)


def steps_of(stream_key, dims, pieces, low, largest):
    factor_of, own = 1.0, jax.random.fold_in(stream_key, 6)
    for dim, shards_of in pieces:
        heights = jnp.exp(jax.random.uniform(jax.random.fold_in(own, dim), (shards_of,), jnp.float32, low / len(pieces), largest / len(pieces)))
        factor_of = factor_of * jnp.repeat(heights, dims[dim] // shards_of).reshape([-1 if axis == dim else 1 for axis in range(len(dims))])
    return factor_of


def setup_inputs(seed: int = 0) -> dict:
    streams_of = jax.random.split(jax.random.key(seed), 7)
    return {
        "source_latent": draw_source_latent(jax.random.fold_in(streams_of[6], 71), 0),
        "target_latent": draw_target_latent(jax.random.fold_in(streams_of[6], 71), 0),
        "log_source_mass": jnp.clip(jax.random.uniform(streams_of[2], (NS,), jnp.float32, -2.0, 2.0) * steps_of(streams_of[2], (NS,), ((0, 8),), -0.4, 0.0), -2.0, 2.0),
        "log_target_mass": jnp.clip(jax.random.uniform(streams_of[3], (NT,), jnp.float32, -2.0, 2.0) * steps_of(streams_of[3], (NT,), ((0, 32),), -0.4, 0.0), -2.0, 2.0).astype(jnp.bfloat16),
        "target_coords": jnp.clip(jax.random.uniform(streams_of[4], (2, NT), jnp.float32, -2.0, 2.0) * steps_of(streams_of[4], (2, NT), ((1, 32),), -0.4, 0.0), -2.0, 2.0).astype(jnp.bfloat16),
        "support": draw_support(jax.random.fold_in(streams_of[6], 71), 0),
    }


EPS = 0.1
NEG = -1.0e30


def reference(source_latent, target_latent, log_source_mass, log_target_mass, target_coords, support):
    source_blocks = jnp.transpose(source_latent.astype(jnp.float32).reshape(LAT, NRB, BLK), (1, 0, 2))
    target_blocks = target_latent.astype(jnp.float32).reshape(LAT, NTB, BLK)
    source_norm = jnp.sum(jnp.square(source_latent.astype(jnp.float32)), axis=0).reshape(NRB, BLK)
    target_norm = jnp.sum(jnp.square(target_latent.astype(jnp.float32)), axis=0).reshape(NTB, BLK)
    source_log = log_source_mass.astype(jnp.float32).reshape(NRB, BLK)
    target_log = log_target_mass.astype(jnp.float32).reshape(NTB, BLK)
    coord_blocks = target_coords.astype(jnp.float32).reshape(2, NTB, BLK)
    block_index = jnp.arange(NRB, dtype=jnp.int32)

    def costs_of(row_block):
        listed = support[row_block]
        right_rows = target_blocks[:, listed, :]
        inner_prod = jnp.einsum("di,dkj->ikj", source_blocks[row_block], right_rows, precision=lax.Precision.HIGHEST)
        cost_tile = (source_norm[row_block][:, None, None] + target_norm[listed][None, :, :] - 2.0 * inner_prod) / LAT
        return listed, cost_tile

    def source_update(target_potential):
        def one_block(row_block):
            listed, cost_tile = costs_of(row_block)
            scores = (target_potential[listed][None, :, :] - cost_tile) / EPS
            highest = jnp.max(scores, axis=(1, 2))
            total_sum = jnp.sum(jnp.exp(scores - highest[:, None, None]), axis=(1, 2))
            return EPS * (source_log[row_block] - highest - jnp.log(total_sum))
        return lax.map(one_block, block_index)

    def target_update(source_potential):
        def scan_step(running, row_block):
            best_all, total_all = running
            listed, cost_tile = costs_of(row_block)
            scores = (source_potential[row_block][:, None, None] - cost_tile) / EPS
            column_best = jnp.max(scores, axis=0)
            old_best = best_all[listed]
            new_best = jnp.maximum(old_best, column_best)
            added_sum = jnp.sum(jnp.exp(scores - new_best[None, :, :]), axis=0)
            total_all = total_all.at[listed].set(total_all[listed] * jnp.exp(old_best - new_best) + added_sum)
            best_all = best_all.at[listed].set(new_best)
            return (best_all, total_all), None
        initial = (jnp.full((NTB, BLK), NEG, jnp.float32), jnp.zeros((NTB, BLK), jnp.float32))
        (best_all, total_all), _ = lax.scan(scan_step, initial, block_index)
        return EPS * (target_log - best_all - jnp.log(total_all))

    target_potential = jnp.zeros((NTB, BLK), jnp.float32)
    source_potential = jnp.zeros((NRB, BLK), jnp.float32)
    for sweep_index in range(ITERS):
        source_potential = source_update(target_potential)
        target_potential = target_update(source_potential)

    def project_block(row_block):
        listed, cost_tile = costs_of(row_block)
        scores = (source_potential[row_block][:, None, None] + target_potential[listed][None, :, :] - cost_tile) / EPS
        highest = jnp.max(scores, axis=(1, 2))
        weights = jnp.exp(scores - highest[:, None, None])
        total_sum = jnp.sum(weights, axis=(1, 2))
        numerator = jnp.einsum("ikj,ckj->ci", weights, coord_blocks[:, listed, :], precision=lax.Precision.HIGHEST)
        return numerator / total_sum[None, :]

    mapped = lax.map(project_block, block_index)
    mapped = jnp.transpose(mapped, (1, 0, 2)).reshape(2, NS)
    return source_potential.reshape(NS), target_potential.reshape(NT), mapped
```

```python
import jax
import jax.numpy as jnp
from jax import lax
from jax.experimental import pallas as pl
from jax.experimental.pallas import tpu as pltpu
from jax.sharding import PartitionSpec as P

LAT = 64
BLK = 128
ITERS = 2
NEG = -1e30
LN2 = 0.6931471805599453
KAPPA = 0.3125 / LN2
UNROLL = 4
MAX_TILES = 192
SLOTS = 256


COL_STEPS = (1, 2, 6, 8, 24)


def both_ways(pairs):
    return [(a, b) for a, b in pairs] + [(b, a) for a, b in pairs]


ROW_STEPS = (
    both_ways([(0, 1), (2, 3), (4, 5), (6, 7)]),
    both_ways([(1, 2), (3, 4), (5, 6), (7, 0)]),
    both_ways([(0, 3), (1, 6), (2, 5), (7, 4)]),
)


def join(a, b):
    return jnp.maximum(a, b) + jnp.log2(1.0 + jnp.exp2(-jnp.abs(a - b)))


def join_cols(x):
    for step in COL_STEPS:
        x = join(x, lax.ppermute(x, "col", [(i, i ^ step) for i in range(32)]))
    return x


def join_rows(x):
    for pairs in ROW_STEPS:
        x = join(x, lax.ppermute(x, "row", pairs))
    return x


def pieces(a):
    hi = a.astype(jnp.bfloat16)
    rest = a - hi.astype(jnp.float32)
    mid = rest.astype(jnp.bfloat16)
    low = (rest - mid.astype(jnp.float32)).astype(jnp.bfloat16)
    return hi, mid, low


def one_rows():
    row = lax.broadcasted_iota(jnp.int32, (BLK - LAT, BLK), 0)
    return jnp.where(row < 3, 1.0, 0.0).astype(jnp.bfloat16)


def side_rows(bias):
    hi, mid, low = (p.astype(jnp.float32) for p in pieces(bias))
    row = lax.broadcasted_iota(jnp.int32, (BLK - LAT, BLK), 0)
    full = jnp.where(row == 0, hi, jnp.where(row == 1, mid, jnp.where(row == 2, low, 0.0)))
    return full.astype(jnp.bfloat16)


def source_block(x_ref, ib):
    return x_ref[ib]


def target_block(y_ref, jb):
    return y_ref[:, pl.ds(pl.multiple_of(jb * BLK, BLK), BLK)]


def dot(lhs, rhs):
    return jnp.dot(lhs, rhs, preferred_element_type=jnp.float32)


def sweep(count_ref, body):
    turns = (count_ref[0] + (UNROLL - 1)) // UNROLL
    lax.fori_loop(0, turns, lambda g, c: (body(g * UNROLL), c)[1], 0)


def fold_into(index, m, s, m_ref, s_ref):
    old = m_ref[index]
    new = jnp.maximum(old, m)
    s_ref[index] = s_ref[index] * jnp.exp2((old - new) * KAPPA) + s * jnp.exp2((m - new) * KAPPA)
    m_ref[index] = new


def finish(m, s):
    top = jnp.max(m, axis=1)
    total = jnp.sum(s * jnp.exp2((m - top[:, None, :]) * KAPPA), axis=1)
    return jnp.where(total > 0.0, top * KAPPA + jnp.log2(total), NEG)


def partial_stats(acc):
    split = acc.reshape(BLK // 8, 8, BLK)
    m = jnp.max(split, axis=0)
    return m, jnp.sum(jnp.exp2((split - m[None]) * KAPPA), axis=0)


def fill_targets(y_ref, b_ref, yt_ref, n):
    for jb in range(n):
        block = y_ref[:, jb * BLK : (jb + 1) * BLK]
        yt_ref[jb] = jnp.concatenate([block, side_rows(b_ref[jb : jb + 1, :])], axis=0).T


def row_kernel(count_ref, list_ref, x_ref, y_ref, b_ref, out_ref, yt_ref, m_ref, s_ref):
    n = out_ref.shape[0]
    fill_targets(y_ref, b_ref, yt_ref, b_ref.shape[0])
    m_ref[...] = jnp.full_like(m_ref, NEG)
    s_ref[...] = jnp.zeros_like(s_ref)

    def body(first):
        entries = [list_ref[first + u] for u in range(UNROLL)]
        accs = []
        for e in entries:
            block = source_block(x_ref, jnp.minimum(e >> 5, n - 1))
            rhs = jnp.concatenate([block, one_rows()], axis=0)
            accs.append(dot(yt_ref[e & 15], rhs))
        stats = [partial_stats(acc) for acc in accs]
        for e, (m, s) in zip(entries, stats):
            fold_into(e >> 5, m, s, m_ref, s_ref)

    sweep(count_ref, body)
    out_ref[...] = finish(m_ref[:n], s_ref[:n])


def col_kernel(count_ref, list_ref, x_ref, y_ref, r_ref, mass_ref, out_ref, xt_ref, m_ref, s_ref):
    n = r_ref.shape[0]
    k = out_ref.shape[0]
    m_ref[...] = jnp.full_like(m_ref, NEG)
    s_ref[...] = jnp.zeros_like(s_ref)

    def fill(ib, c):
        a = 3.2 * (mass_ref[pl.ds(ib, 1), :] - LN2 * r_ref[pl.ds(ib, 1), :])
        block = source_block(x_ref, ib)
        xt_ref[ib] = jnp.concatenate([block, side_rows(a)], axis=0).T
        return c

    lax.fori_loop(0, n, fill, 0, unroll=4)

    def body(first):
        entries = [list_ref[first + u] for u in range(UNROLL)]
        accs = []
        for e in entries:
            rhs = jnp.concatenate([target_block(y_ref, e & 15), one_rows()], axis=0)
            accs.append(dot(xt_ref[jnp.minimum(e >> 5, n - 1)], rhs))
        stats = [partial_stats(acc) for acc in accs]
        for e, (m, s) in zip(entries, stats):
            fold_into(e & 31, m, s, m_ref, s_ref)

    sweep(count_ref, body)
    out_ref[...] = finish(m_ref[:k], s_ref[:k])


def project_kernel(
    count_ref, list_ref, x_ref, y_ref, b_ref, coord_ref, out_ref, yt_ref, m_ref, w_ref
):
    n = out_ref.shape[0]
    fill_targets(y_ref, b_ref, yt_ref, b_ref.shape[0])
    m_ref[...] = jnp.full_like(m_ref, NEG)
    w_ref[...] = jnp.zeros_like(w_ref)

    def body(first):
        entries = [list_ref[first + u] for u in range(UNROLL)]
        accs = []
        for e in entries:
            block = source_block(x_ref, jnp.minimum(e >> 5, n - 1))
            rhs = jnp.concatenate([block, one_rows()], axis=0)
            accs.append(dot(yt_ref[e & 15], rhs))
        stats = []
        for e, acc in zip(entries, accs):
            m = jnp.max(acc, axis=0, keepdims=True)
            p = jnp.exp2((acc - m) * KAPPA)
            hi = p.astype(jnp.bfloat16)
            low = (p - hi.astype(jnp.float32)).astype(jnp.bfloat16)
            coords = coord_ref[:, pl.ds(pl.multiple_of((e & 15) * BLK, BLK), BLK)]
            stats.append((m, (dot(coords, hi) + dot(coords, low))[:8]))
        for e, (m, w) in zip(entries, stats):
            index = e >> 5
            old = m_ref[index]
            new = jnp.maximum(old, m)
            w_ref[index] = w_ref[index] * jnp.exp2((old - new) * KAPPA) + w * jnp.exp2((m - new) * KAPPA)
            m_ref[index] = new

    sweep(count_ref, body)
    total = w_ref[:n, 2, :]
    live = total > 0.0
    safe = jnp.where(live, total, 1.0)
    out_ref[:, 0, :] = jnp.where(live, m_ref[:n, 0, :] * KAPPA + jnp.log2(safe), NEG)
    out_ref[:, 1, :] = w_ref[:n, 0, :] / safe
    out_ref[:, 2, :] = w_ref[:n, 1, :] / safe


SMEM = pl.BlockSpec(memory_space=pltpu.SMEM)
VMEM = pl.BlockSpec(memory_space=pltpu.VMEM)
PARAMS = pltpu.CompilerParams(vmem_limit_bytes=32 << 20)


def call(kernel, shape, scratch, smem_count, args):
    return pl.pallas_call(
        kernel,
        out_shape=jax.ShapeDtypeStruct(shape, jnp.float32),
        in_specs=[SMEM] * smem_count + [VMEM] * (len(args) - smem_count),
        out_specs=VMEM,
        scratch_shapes=scratch,
        compiler_params=PARAMS,
    )(*args)


def tile_list(support, per_shard, here):
    rows, per_list = support.shape
    local = support - here * per_shard
    owned = (local >= 0) & (local < per_shard)
    flags = owned.astype(jnp.float32)
    upto = (jnp.arange(per_list)[:, None] <= jnp.arange(per_list)[None, :]).astype(jnp.float32)
    before = (jnp.arange(rows)[None, :] < jnp.arange(rows)[:, None]).astype(jnp.float32)
    within = flags @ upto
    start = before @ within[:, -1:]
    place = jnp.where(owned, (within + start).astype(jnp.int32) - 1, -1)
    count = jnp.sum(owned.astype(jnp.int32)).reshape(1)
    code = jnp.arange(rows, dtype=jnp.int32)[:, None] * 32 + local
    slot = jnp.arange(SLOTS, dtype=jnp.int32)
    listed = jnp.sum(
        jnp.where(place[:, :, None] == slot, code[:, :, None], 0), axis=(0, 1), dtype=jnp.int32
    )
    return count, jnp.where(slot < count, listed, rows * 32 + per_shard)


def on_device(
    source_latent, target_latent, log_source_mass, log_target_mass, target_coords, support
):
    cols = lax.axis_size("col")
    here = lax.axis_index("col")
    n = support.shape[0]
    k = target_latent.shape[1] // BLK
    mine = n // cols
    bf16, f32 = jnp.bfloat16, jnp.float32

    own = source_latent.reshape(LAT, mine, BLK).transpose(1, 0, 2)
    spread = jnp.broadcast_to(own[None], (cols,) + own.shape)
    x = lax.all_to_all(spread, "col", 0, 0).reshape(n, LAT, BLK)

    count, tiles = tile_list(support, k, here)
    y = target_latent
    y_half = 0.5 * jnp.sum(jnp.square(y.astype(f32)), axis=0).reshape(k, BLK)
    source_log = log_source_mass.reshape(n, BLK)
    target_log = log_target_mass.astype(f32).reshape(k, BLK)
    ones = jnp.ones((1, k * BLK), bf16)
    coords = jnp.concatenate([target_coords, ones, jnp.zeros((13, k * BLK), bf16)], axis=0)

    row_scratch = [
        pltpu.VMEM((k, BLK, BLK), bf16),
        pltpu.VMEM((n + 1, 8, BLK), f32),
        pltpu.VMEM((n + 1, 8, BLK), f32),
    ]
    col_scratch = [
        pltpu.VMEM((n, BLK, BLK), bf16),
        pltpu.VMEM((k + 1, 8, BLK), f32),
        pltpu.VMEM((k + 1, 8, BLK), f32),
    ]
    b = -y_half
    for _ in range(ITERS):
        r = call(row_kernel, (n, BLK), row_scratch, 2, (count, tiles, x, y, b))
        r = join_cols(r)
        c = call(col_kernel, (k, BLK), col_scratch, 2, (count, tiles, x, y, r, source_log))
        c = join_rows(c)
        b = 3.2 * (target_log - LN2 * c)
    project_scratch = [
        pltpu.VMEM((k, BLK, BLK), bf16),
        pltpu.VMEM((n + 1, 1, BLK), f32),
        pltpu.VMEM((n + 1, 8, BLK), f32),
    ]
    part = call(project_kernel, (n, 3, BLK), project_scratch, 2, (count, tiles, x, y, b, coords))
    part = lax.all_to_all(part.reshape(cols, mine, 3, BLK), "col", 0, 0)
    level = part[:, :, 0]
    weight = jnp.exp2(level - jnp.max(level, axis=0))
    mapped = jnp.sum(weight[:, :, None] * part[:, :, 1:], axis=0) / jnp.sum(weight, axis=0)[:, None]
    mapped = mapped.transpose(1, 0, 2).reshape(2, mine * BLK)

    own_r = lax.dynamic_slice_in_dim(r, here * mine, mine)
    own_log = lax.dynamic_slice_in_dim(source_log, here * mine, mine)
    x_half = 0.5 * jnp.sum(jnp.square(source_latent.astype(f32)), axis=0)
    out_source = (3.2 * (own_log - LN2 * own_r).reshape(-1) + x_half) / 32.0
    out_target = ((b + y_half) / 32.0).reshape(-1)
    return out_source, out_target, mapped


def solution(mesh):
    in_specs = (
        P(None, ("row", "col")),
        P(None, "col"),
        P("row"),
        P("col"),
        P(None, "col"),
        P("row", None),
    )
    out_specs = (P(("row", "col")), P("col"), P(None, ("row", "col")))
    return jax.shard_map(
        on_device, mesh=mesh, in_specs=in_specs, out_specs=out_specs, check_vma=False
    )
```

```python
import jax
import jax.numpy as jnp
from jax import lax
from jax.experimental import pallas as pl
from jax.experimental.pallas import tpu as pltpu
from jax.sharding import PartitionSpec as P

LAT = 64
BLK = 128
ITERS = 2
NEG = -1e30
LN2 = 0.6931471805599453
KAPPA = 0.3125 / LN2
UNROLL = 32
PACK = 80


def chip_groups(cols):
    return [[c for c in range(cols) if c % 2 == core] for core in range(2)]


def stack_groups(rows, cols):
    return [
        [r * cols + 2 * chip + core for r in range(rows) for core in range(2)]
        for chip in range(cols // 2)
    ]


def exchange(x, axis, groups):
    return lax.all_to_all(x, axis, 0, 0, axis_index_groups=groups)


def join(parts):
    top = jnp.max(parts, axis=0)
    return top + jnp.log2(jnp.sum(jnp.exp2(parts - top[None]), axis=0))


def bias_of(mass, level):
    return 3.2 * (mass - LN2 * level)


def pieces(a):
    hi = a.astype(jnp.bfloat16)
    rest = a - hi.astype(jnp.float32)
    mid = rest.astype(jnp.bfloat16)
    low = (rest - mid.astype(jnp.float32)).astype(jnp.bfloat16)
    return hi, mid, low


def one_rows():
    row = lax.broadcasted_iota(jnp.int32, (BLK - LAT, BLK), 0)
    return jnp.where(row < 3, 1.0, 0.0).astype(jnp.bfloat16)


def side_rows(bias):
    hi, mid, low = (p.astype(jnp.float32) for p in pieces(bias))
    row = lax.broadcasted_iota(jnp.int32, (BLK - LAT, BLK), 0)
    full = jnp.where(row == 0, hi, jnp.where(row == 1, mid, jnp.where(row == 2, low, 0.0)))
    return full.astype(jnp.bfloat16)


def columns(jb):
    return pl.ds(pl.multiple_of(jb * BLK, BLK), BLK)


def dot(lhs, rhs):
    return jnp.dot(lhs, rhs, preferred_element_type=jnp.float32)


def sweep(count_ref, list_ref, body):
    def turn(g, c):
        body([list_ref[g * UNROLL + u] for u in range(UNROLL)])
        return c

    lax.fori_loop(0, (count_ref[0] + (UNROLL - 1)) // UNROLL, turn, 0)


def source_of(e):
    return e >> 6


def target_of(e):
    return e & 63


def fold_into(index, m, s, m_ref, s_ref):
    old = m_ref[index]
    new = jnp.maximum(old, m)
    s_ref[index] = s_ref[index] * jnp.exp2((old - new) * KAPPA) + s * jnp.exp2((m - new) * KAPPA)
    m_ref[index] = new


def finish(m, s):
    top = jnp.max(m, axis=1)
    total = jnp.sum(s * jnp.exp2((m - top[:, None, :]) * KAPPA), axis=1)
    return jnp.where(total > 0.0, top * KAPPA + jnp.log2(total), NEG)


def partial_stats(acc):
    split = acc.reshape(BLK // 8, 8, BLK)
    m = jnp.max(split, axis=0)
    return m, jnp.sum(jnp.exp2((split - m[None]) * KAPPA), axis=0)


def clear(m_ref, s_ref):
    m_ref[...] = jnp.full_like(m_ref, NEG)
    s_ref[...] = jnp.zeros_like(s_ref)


def fill_targets(pack_ref, b, yt_ref):
    for jb in range(yt_ref.shape[0]):
        block = pack_ref[:LAT, jb * BLK : (jb + 1) * BLK]
        yt_ref[jb] = jnp.concatenate([block, side_rows(b[jb : jb + 1, :])], axis=0).T


def target_by_source(entries, x_ref, yt_ref):
    ones = one_rows()
    last = x_ref.shape[0] - 1
    return [
        dot(
            yt_ref[target_of(e) & 31],
            jnp.concatenate([x_ref[jnp.minimum(source_of(e), last)], ones], axis=0),
        )
        for e in entries
    ]


def row_sweep(count_ref, list_ref, x_ref, pack_ref, b, out_ref, yt_ref, m_ref, s_ref):
    fill_targets(pack_ref, b, yt_ref)
    clear(m_ref, s_ref)

    def body(entries):
        stats = [partial_stats(acc) for acc in target_by_source(entries, x_ref, yt_ref)]
        for e, (m, s) in zip(entries, stats):
            fold_into(source_of(e), m, s, m_ref, s_ref)

    sweep(count_ref, list_ref, body)
    n = x_ref.shape[0]
    out_ref[...] = jnp.broadcast_to(finish(m_ref[:n], s_ref[:n])[None], out_ref.shape)


def first_row_kernel(count_ref, list_ref, x_ref, pack_ref, b_ref, out_ref, yt_ref, m_ref, s_ref):
    row_sweep(count_ref, list_ref, x_ref, pack_ref, b_ref[...], out_ref, yt_ref, m_ref, s_ref)


def row_kernel(
    count_ref, list_ref, x_ref, pack_ref, c_ref, mass_ref, out_ref, yt_ref, m_ref, s_ref
):
    b = bias_of(mass_ref[...], join(c_ref[...]))
    row_sweep(count_ref, list_ref, x_ref, pack_ref, b, out_ref, yt_ref, m_ref, s_ref)


def col_kernel(
    count_ref, list_ref, x_ref, pack_ref, r_ref, mass_ref, out_ref, xt_ref, m_ref, s_ref
):
    n = x_ref.shape[0]
    a = bias_of(mass_ref[...], join(r_ref[...]))
    for ib in range(n):
        xt_ref[ib] = jnp.concatenate([x_ref[ib], side_rows(a[ib : ib + 1, :])], axis=0).T
    clear(m_ref, s_ref)

    def body(entries):
        ones = one_rows()
        accs = [
            dot(
                xt_ref[jnp.minimum(source_of(e), n - 1)],
                jnp.concatenate([pack_ref[:LAT, columns(target_of(e) & 31)], ones], axis=0),
            )
            for e in entries
        ]
        stats = [partial_stats(acc) for acc in accs]
        for e, (m, s) in zip(entries, stats):
            fold_into(target_of(e), m, s, m_ref, s_ref)

    sweep(count_ref, list_ref, body)
    k = m_ref.shape[0] - 1
    out_ref[...] = jnp.broadcast_to(finish(m_ref[:k], s_ref[:k])[None], out_ref.shape)


def project_kernel(
    count_ref, list_ref, x_ref, pack_ref, c_ref, mass_ref, out_ref, yt_ref, m_ref, w_ref
):
    b = bias_of(mass_ref[...], join(c_ref[...]))
    fill_targets(pack_ref, b, yt_ref)
    clear(m_ref, w_ref)

    def body(entries):
        stats = []
        for e, acc in zip(entries, target_by_source(entries, x_ref, yt_ref)):
            m = jnp.max(acc, axis=0, keepdims=True)
            p = jnp.exp2((acc - m) * KAPPA)
            hi = p.astype(jnp.bfloat16)
            low = (p - hi.astype(jnp.float32)).astype(jnp.bfloat16)
            side = pack_ref[LAT:, columns(target_of(e) & 31)]
            stats.append((m, (dot(side, hi) + dot(side, low))[:8]))
        for e, (m, w) in zip(entries, stats):
            fold_into(source_of(e), m, w, m_ref, w_ref)

    sweep(count_ref, list_ref, body)
    out_ref[...] = jnp.zeros_like(out_ref)
    for ib in range(x_ref.shape[0]):
        w = w_ref[ib]
        total = w[2:3]
        live = total > 0.0
        safe = jnp.where(live, total, 1.0)
        half = ib % 2
        out_ref[ib // 2, half : half + 1, :] = jnp.where(
            live, m_ref[ib] * KAPPA + jnp.log2(safe), NEG
        )
        out_ref[ib // 2, 2 + half : 3 + half, :] = w[0:1] / safe
        out_ref[ib // 2, 4 + half : 5 + half, :] = w[1:2] / safe


SMEM = pl.BlockSpec(memory_space=pltpu.SMEM)
VMEM = pl.BlockSpec(memory_space=pltpu.VMEM)


def call(kernel, shape, scratch, count, tiles, *args):
    return pl.pallas_call(
        kernel,
        out_shape=jax.ShapeDtypeStruct(shape, jnp.float32),
        in_specs=[SMEM] * 2 + [VMEM] * len(args),
        out_specs=VMEM,
        scratch_shapes=scratch,
        compiler_params=pltpu.CompilerParams(vmem_limit_bytes=32 << 20),
    )(count, tiles, *args)


def tile_list(support, chip, per_chip, slots):
    rows, per_list = support.shape
    owned = support // per_chip == chip
    flags = owned.astype(jnp.float32)
    upto = (jnp.arange(per_list)[:, None] <= jnp.arange(per_list)[None, :]).astype(jnp.float32)
    before = (jnp.arange(rows)[None, :] < jnp.arange(rows)[:, None]).astype(jnp.float32)
    within = flags @ upto
    start = before @ within[:, -1:]
    place = jnp.where(owned, (within + start).astype(jnp.int32) - 1, -1)
    count = jnp.sum(owned.astype(jnp.int32)).reshape(1)
    code = jnp.arange(rows, dtype=jnp.int32)[:, None] * 64 + support % per_chip
    slot = jnp.arange(slots, dtype=jnp.int32)
    listed = jnp.sum(
        jnp.where(place[:, :, None] == slot, code[:, :, None], 0), axis=(0, 1), dtype=jnp.int32
    )
    return count, jnp.where(slot < count, listed, rows * 64 + per_chip)


def on_device(
    source_latent, target_latent, log_source_mass, log_target_mass, target_coords, support
):
    rows, cols = lax.axis_size("row"), lax.axis_size("col")
    here = lax.axis_index("col")
    chip, core = here // 2, here % 2
    chips = cols // 2
    mine = support.shape[0] // cols
    own_k = target_latent.shape[1] // BLK
    n, k = chips * mine, 2 * own_k
    bf16, f32 = jnp.bfloat16, jnp.float32
    by_chip, by_stack = chip_groups(cols), stack_groups(rows, cols)

    def of_core(a):
        split = a.reshape((chips, 2, mine) + a.shape[1:])
        split = jnp.where(core == 0, split[:, 0], split[:, 1])
        return split.reshape((n,) + a.shape[1:])

    own = source_latent.reshape(LAT, mine, BLK).transpose(1, 0, 2)
    spread = jnp.broadcast_to(own[None], (chips,) + own.shape)
    x = exchange(spread, "col", by_chip).reshape(n, LAT, BLK)

    width = target_latent.shape[1]
    pack = jnp.concatenate(
        [
            target_latent,
            target_coords,
            jnp.ones((1, width), bf16),
            log_target_mass[None],
            jnp.zeros((PACK - LAT - 4, width), bf16),
        ],
        axis=0,
    )
    other = lax.ppermute(pack, "col", [(i, i ^ 1) for i in range(cols)])
    pack = jnp.concatenate(
        [jnp.where(core == 0, pack, other), jnp.where(core == 0, other, pack)], axis=1
    )
    y_half = 0.5 * jnp.sum(jnp.square(pack[:LAT].astype(f32)), axis=0).reshape(k, BLK)
    target_log = pack[LAT + 3].astype(f32).reshape(k, BLK)
    source_log = of_core(log_source_mass.reshape(-1, BLK))
    count, tiles = tile_list(of_core(support), chip, k, 12 * mine * chips)

    stats = [pltpu.VMEM((n + 1, 8, BLK), f32)] * 2
    row_scratch = [pltpu.VMEM((k, BLK, BLK), bf16)] + stats
    col_scratch = [pltpu.VMEM((n, BLK, BLK), bf16)] + [pltpu.VMEM((k + 1, 8, BLK), f32)] * 2
    project_scratch = [
        pltpu.VMEM((k, BLK, BLK), bf16),
        pltpu.VMEM((n + 1, 1, BLK), f32),
        pltpu.VMEM((n + 1, 8, BLK), f32),
    ]
    for sweep_index in range(ITERS):
        to_chips = (chips, n, BLK)
        if sweep_index == 0:
            r = call(first_row_kernel, to_chips, row_scratch, count, tiles, x, pack, -y_half)
        else:
            r = call(row_kernel, to_chips, row_scratch, count, tiles, x, pack, c, target_log)
        r = exchange(r, "col", by_chip)
        c = call(
            col_kernel, (2 * rows, k, BLK), col_scratch, count, tiles, x, pack, r, source_log
        )
        c = exchange(c, ("row", "col"), by_stack)
    part = call(
        project_kernel, (chips, 8, BLK), project_scratch, count, tiles, x, pack, c, target_log
    )
    part = exchange(part, "col", by_chip)
    level = part[:, :mine]
    weight = jnp.exp2(level - jnp.max(level, axis=0))
    bottom = jnp.sum(weight, axis=0)
    mapped = jnp.stack(
        [
            jnp.sum(weight * part[:, (q + 1) * mine : (q + 2) * mine], axis=0) / bottom
            for q in range(2)
        ]
    ).reshape(2, mine * BLK)

    own_r = join(lax.dynamic_slice_in_dim(r, chip * mine, mine, 1))
    own_log = lax.dynamic_slice_in_dim(source_log, chip * mine, mine)
    x_half = 0.5 * jnp.sum(jnp.square(source_latent.astype(f32)), axis=0)
    out_source = (bias_of(own_log, own_r).reshape(-1) + x_half) / 32.0
    b = bias_of(target_log, join(c))
    out_target = lax.dynamic_slice_in_dim((b + y_half) / 32.0, core * own_k, own_k).reshape(-1)
    return out_source, out_target, mapped


def solution(mesh):
    in_specs = (
        P(None, ("row", "col")),
        P(None, "col"),
        P("row"),
        P("col"),
        P(None, "col"),
        P("row", None),
    )
    out_specs = (P(("row", "col")), P("col"), P(None, ("row", "col")))
    return jax.shard_map(
        on_device, mesh=mesh, in_specs=in_specs, out_specs=out_specs, check_vma=False
    )
```

```python
import functools

import jax
import jax.numpy as jnp
from jax import lax
from jax.experimental import pallas as pl
from jax.experimental.pallas import tpu as pltpu
from jax.sharding import PartitionSpec as P

LAT = 64
BLK = 128
ITERS = 2
NEG = -1e30
LN2 = 0.6931471805599453
KAPPA = 0.3125 / LN2
UNROLL = 32
PACK = 80
GROUP = 16


def chip_groups(cols):
    return [[c for c in range(cols) if c % 2 == core] for core in range(2)]


def swap_cores(x, cols):
    return lax.ppermute(x, "col", [(i, i ^ 1) for i in range(cols)])


def exchange(x, axis, groups=None):
    return lax.all_to_all(x, axis, 0, 0, axis_index_groups=groups)


def join(parts):
    top = jnp.max(parts, axis=0)
    return top + jnp.log2(jnp.sum(jnp.exp2(parts - top[None]), axis=0))


def join_pair(a, b):
    return jnp.maximum(a, b) + jnp.log2(1.0 + jnp.exp2(-jnp.abs(a - b)))


def bias_of(mass, level):
    return 3.2 * (mass - LN2 * level)


def pieces(a):
    hi = a.astype(jnp.bfloat16)
    rest = a - hi.astype(jnp.float32)
    mid = rest.astype(jnp.bfloat16)
    low = (rest - mid.astype(jnp.float32)).astype(jnp.bfloat16)
    return hi, mid, low


def fill_hot(hot_ref):
    row = lax.broadcasted_iota(jnp.int32, (BLK - LAT, BLK), 0)
    for q in range(GROUP):
        hit = ((row & (GROUP - 1)) == q) & (row < 3 * GROUP)
        hot_ref[q] = jnp.where(hit, 1.0, 0.0).astype(jnp.bfloat16)


def fill_biased(plain_ref, bias, full_ref):
    for first in range(0, plain_ref.shape[0], GROUP):
        hi, mid, low = pieces(bias[first : first + GROUP])
        blank = jnp.zeros((LAT, BLK), jnp.bfloat16)
        side = jnp.concatenate([blank, hi, mid, low, blank[:GROUP]], axis=0).T
        for block in range(first, first + GROUP):
            full_ref[block] = plain_ref[block] + side


def columns(jb):
    return pl.ds(pl.multiple_of(jb * BLK, BLK), BLK)


def dot(lhs, rhs):
    return jnp.dot(lhs, rhs, preferred_element_type=jnp.float32)


def sweep(list_ref, body):
    last_row = list_ref.shape[0] - 1
    turns = (list_ref[last_row, 0] + (UNROLL - 1)) // UNROLL
    per_row = BLK // UNROLL

    def turn(g, c):
        row, start = g // per_row, (g % per_row) * UNROLL
        body([list_ref[row, start + u] for u in range(UNROLL)])
        return c

    lax.fori_loop(0, turns, turn, 0)


def source_of(e):
    return e >> 6


def target_of(e):
    return e & 63


def fold_into(index, m, s, m_ref, s_ref):
    old = m_ref[index]
    new = jnp.maximum(old, m)
    s_ref[index] = s_ref[index] * jnp.exp2((old - new) * KAPPA) + s * jnp.exp2((m - new) * KAPPA)
    m_ref[index] = new


def finish(m, s):
    top = jnp.max(m, axis=1)
    total = jnp.sum(s * jnp.exp2((m - top[:, None, :]) * KAPPA), axis=1)
    return jnp.where(total > 0.0, top * KAPPA + jnp.log2(total), NEG)


def partial_stats(acc):
    split = acc.reshape(BLK // 8, 8, BLK)
    m = jnp.max(split, axis=0)
    return m, jnp.sum(jnp.exp2((split - m[None]) * KAPPA), axis=0)


def clear(m_ref, s_ref):
    m_ref[...] = jnp.full_like(m_ref, NEG)
    s_ref[...] = jnp.zeros_like(s_ref)


def source_block(x_ref, s):
    return x_ref[s >> 1, :, columns(s & 1)]


def target_by_source(entries, x_ref, yt_ref, hot_ref):
    last = 2 * x_ref.shape[0] - 1
    return [
        dot(
            yt_ref[target_of(e) & 31],
            jnp.concatenate(
                [source_block(x_ref, jnp.minimum(source_of(e), last)), hot_ref[e & (GROUP - 1)]],
                axis=0,
            ),
        )
        for e in entries
    ]


def transposed(block):
    return jnp.concatenate([block, jnp.zeros_like(block)], axis=0).T


def target_side_kernel(pack_ref, yt0_ref, minus_half_ref):
    for q in range(yt0_ref.shape[0]):
        block = pack_ref[:LAT, q * BLK : (q + 1) * BLK]
        yt0_ref[q] = transposed(block)
        minus_half_ref[q : q + 1, :] = -0.5 * jnp.sum(
            jnp.square(block.astype(jnp.float32)), axis=0, keepdims=True
        )


def spread_kernel(in_ref, out_ref):
    out_ref[...] = jnp.broadcast_to(in_ref[...][None], out_ref.shape)


def source_side_kernel(x_ref, xt0_ref):
    for q in range(xt0_ref.shape[0]):
        xt0_ref[q] = transposed(x_ref[q // 2, :, (q % 2) * BLK : (q % 2 + 1) * BLK])


def start_copy(from_ref, to_ref, sem):
    copy = pltpu.make_async_copy(from_ref, to_ref, sem)
    copy.start()
    return copy


def first_row_kernel(tiles_ref, b_ref, x_ref, yt0_ref, out_ref, list_ref, mass_ref, sems, *scratch):
    copy = start_copy(tiles_ref, list_ref, sems.at[0])
    row_pass(copy, list_ref, x_ref, yt0_ref, lambda: b_ref[...], out_ref, *scratch)


def row_kernel(
    tiles_ref, log_ref, x_ref, yt0_ref, c_ref, d_ref, out_ref, list_ref, mass_ref, sems, *scratch
):
    copy = start_copy(tiles_ref, list_ref, sems.at[0])
    mass = start_copy(log_ref, mass_ref, sems.at[1])

    def bias():
        level = join_pair(c_ref[...], d_ref[...])
        mass.wait()
        return bias_of(mass_ref[...], level)

    row_pass(copy, list_ref, x_ref, yt0_ref, bias, out_ref, *scratch)


def row_pass(copy, list_ref, x_ref, yt0_ref, bias, out_ref, yt_ref, hot_ref, m_ref, s_ref):
    fill_hot(hot_ref)
    clear(m_ref, s_ref)
    fill_biased(yt0_ref, bias(), yt_ref)
    copy.wait()

    def body(entries):
        stats = [partial_stats(a) for a in target_by_source(entries, x_ref, yt_ref, hot_ref)]
        for e, (m, s) in zip(entries, stats):
            fold_into(source_of(e), m, s, m_ref, s_ref)

    sweep(list_ref, body)
    n = m_ref.shape[0] - 1
    out_ref[...] = jnp.broadcast_to(finish(m_ref[:n], s_ref[:n])[None], out_ref.shape)


def col_kernel(
    tiles_ref, log_ref, xt0_ref, pack_ref, r_ref, out_ref, list_ref, mass_ref, sems, xt_ref, hot_ref, m_ref, s_ref
):
    copy = start_copy(tiles_ref, list_ref, sems.at[0])
    mass = start_copy(log_ref, mass_ref, sems.at[1])
    n = xt0_ref.shape[0]
    fill_hot(hot_ref)
    clear(m_ref, s_ref)
    level = join(r_ref[...])
    mass.wait()
    fill_biased(xt0_ref, bias_of(mass_ref[...], level), xt_ref)
    copy.wait()

    def body(entries):
        accs = []
        for e in entries:
            block = pack_ref[:LAT, columns(target_of(e) & 31)]
            rhs = jnp.concatenate([block, hot_ref[source_of(e) & (GROUP - 1)]], axis=0)
            accs.append(dot(xt_ref[jnp.minimum(source_of(e), n - 1)], rhs))
        stats = [partial_stats(acc) for acc in accs]
        for e, (m, s) in zip(entries, stats):
            fold_into(target_of(e), m, s, m_ref, s_ref)

    sweep(list_ref, body)
    k = m_ref.shape[0] - 1
    out_ref[...] = jnp.broadcast_to(finish(m_ref[:k], s_ref[:k])[None], out_ref.shape)


def project_kernel(
    tiles_ref, log_ref, x_ref, yt0_ref, pack_ref, c_ref, d_ref, out_ref, list_ref, mass_ref, sems, yt_ref, hot_ref, m_ref, w_ref
):
    copy = start_copy(tiles_ref, list_ref, sems.at[0])
    mass = start_copy(log_ref, mass_ref, sems.at[1])
    fill_hot(hot_ref)
    clear(m_ref, w_ref)
    level = join_pair(c_ref[...], d_ref[...])
    mass.wait()
    fill_biased(yt0_ref, bias_of(mass_ref[...], level), yt_ref)
    copy.wait()

    def body(entries):
        stats = []
        for e, acc in zip(entries, target_by_source(entries, x_ref, yt_ref, hot_ref)):
            m = jnp.max(acc, axis=0, keepdims=True)
            p = jnp.exp2((acc - m) * KAPPA)
            hi = p.astype(jnp.bfloat16)
            low = (p - hi.astype(jnp.float32)).astype(jnp.bfloat16)
            side = pack_ref[LAT:, columns(target_of(e) & 31)]
            both = jnp.concatenate([hi, low], axis=0)
            stats.append((m, dot(jnp.concatenate([side, side], axis=1), both)[:8]))
        for e, (m, w) in zip(entries, stats):
            fold_into(source_of(e), m, w, m_ref, w_ref)

    sweep(list_ref, body)
    out_ref[...] = jnp.zeros_like(out_ref)
    for ib in range(2 * x_ref.shape[0]):
        w = w_ref[ib]
        total = w[2:3]
        live = total > 0.0
        safe = jnp.where(live, total, 1.0)
        half = ib % 2
        out_ref[ib // 2, half : half + 1, :] = jnp.where(
            live, m_ref[ib] * KAPPA + jnp.log2(safe), NEG
        )
        out_ref[ib // 2, 2 + half : 3 + half, :] = w[0:1] / safe
        out_ref[ib // 2, 4 + half : 5 + half, :] = w[1:2] / safe


VMEM = pl.BlockSpec(memory_space=pltpu.VMEM)
HBM = pl.BlockSpec(memory_space=pltpu.HBM)


def call(kernel, outs, scratch, far, near):
    put = pltpu.with_memory_space_constraint
    return pl.pallas_call(
        kernel,
        out_shape=outs,
        in_specs=[HBM] * len(far) + [VMEM] * len(near),
        out_specs=jax.tree.map(lambda _: VMEM, outs),
        scratch_shapes=scratch,
        compiler_params=pltpu.CompilerParams(vmem_limit_bytes=16 << 20),
    )(*(put(a, pltpu.HBM) for a in far), *(put(a, pltpu.VMEM) for a in near))


def tile_list(support, chip, per_chip, slots):
    rows, per_list = support.shape
    owned = support // per_chip == chip
    flags = owned.astype(jnp.float32)
    upto = (jnp.arange(per_list)[:, None] <= jnp.arange(per_list)[None, :]).astype(jnp.float32)
    before = (jnp.arange(rows)[None, :] < jnp.arange(rows)[:, None]).astype(jnp.float32)
    within = flags @ upto
    start = before @ within[:, -1:]
    place = jnp.where(owned, (within + start).astype(jnp.int32) - 1, -1)
    count = jnp.sum(owned.astype(jnp.int32))
    code = jnp.arange(rows, dtype=jnp.int32)[:, None] * 64 + support % per_chip
    slot = jnp.arange(slots, dtype=jnp.int32)
    listed = jnp.sum(
        jnp.where(place[:, :, None] == slot, code[:, :, None], 0), axis=(0, 1), dtype=jnp.int32
    )
    listed = jnp.where(slot < count, listed, rows * 64 + per_chip)
    return jnp.concatenate([listed, jnp.broadcast_to(count, (BLK,))]).reshape(-1, BLK)


def on_device(
    source_latent, target_latent, log_source_mass, log_target_mass, target_coords, support
):
    rows, cols = lax.axis_size("row"), lax.axis_size("col")
    here = lax.axis_index("col")
    chip, core = here // 2, here % 2
    chips = cols // 2
    mine = support.shape[0] // cols
    own_k = target_latent.shape[1] // BLK
    n, k = chips * mine, 2 * own_k
    bf16, f32 = jnp.bfloat16, jnp.float32
    by_chip = chip_groups(cols)

    def of_core(a):
        split = a.reshape((chips, 2, mine) + a.shape[1:])
        split = jnp.where(core == 0, split[:, 0], split[:, 1])
        return split.reshape((n,) + a.shape[1:])

    spread = pl.pallas_call(
        spread_kernel,
        out_shape=jax.ShapeDtypeStruct((chips,) + source_latent.shape, bf16),
        in_specs=[VMEM],
        out_specs=VMEM,
    )(source_latent)
    x = exchange(spread, "col", by_chip)

    def pair(a):
        other = swap_cores(a, cols)
        return jnp.concatenate(
            [jnp.where(core == 0, a, other), jnp.where(core == 0, other, a)], axis=1
        )

    width = 2 * target_latent.shape[1]
    targets = pair(target_latent)
    coords, target_log = pair(target_coords), pair(log_target_mass[None])
    pack = jnp.concatenate(
        [targets, coords, jnp.ones((1, width), bf16), jnp.zeros((PACK - LAT - 3, width), bf16)],
        axis=0,
    )
    target_log = target_log.astype(f32).reshape(k, BLK)
    source_log = of_core(log_source_mass.reshape(-1, BLK))
    tiles = tile_list(of_core(support), chip, k, 12 * mine * chips)

    common = [
        pltpu.SMEM(tiles.shape, jnp.int32),
        pltpu.VMEM((n, BLK), f32),
        pltpu.SemaphoreType.DMA((2,)),
        pltpu.VMEM((n, BLK, BLK), bf16),
        pltpu.VMEM((GROUP, BLK - LAT, BLK), bf16),
    ]
    row_scratch = common + [pltpu.VMEM((n + 1, 8, BLK), f32)] * 2
    col_scratch = common + [pltpu.VMEM((k + 1, 8, BLK), f32)] * 2
    project_scratch = common + [pltpu.VMEM((n + 1, 1, BLK), f32), pltpu.VMEM((n + 1, 8, BLK), f32)]

    tiles, source_log, target_log = lax.optimization_barrier((tiles, source_log, target_log))
    yt0, minus_half = call(
        target_side_kernel,
        [pltpu.VMEM((k, BLK, BLK), bf16), pltpu.VMEM((k, BLK), f32)],
        [],
        [],
        [pack],
    )
    to_chips = jax.ShapeDtypeStruct((chips, n, BLK), f32)
    to_rows = jax.ShapeDtypeStruct((rows, k, BLK), f32)
    for sweep_index in range(ITERS):
        if sweep_index == 0:
            r = call(first_row_kernel, to_chips, row_scratch, [tiles], [minus_half, x, yt0])
            xt0 = call(source_side_kernel, pltpu.VMEM((n, BLK, BLK), bf16), [], [], [x])
        else:
            r = call(row_kernel, to_chips, row_scratch, [tiles, target_log], [x, yt0, c, d])
        r = exchange(r, "col", by_chip)
        c = call(col_kernel, to_rows, col_scratch, [tiles, source_log], [xt0, pack, r])
        c = join(exchange(c, "row"))
        d = swap_cores(c, cols)
    to_owners = jax.ShapeDtypeStruct((chips, 8, BLK), f32)
    part = call(
        project_kernel,
        to_owners,
        project_scratch,
        [tiles, target_log],
        [x, yt0, pack, c, d],
    )
    part, r, source_latent = lax.optimization_barrier((part, r, source_latent))
    part = exchange(part, "col", by_chip)
    level = part[:, :mine]
    weight = jnp.exp2(level - jnp.max(level, axis=0))
    bottom = jnp.sum(weight, axis=0)
    mapped = jnp.stack(
        [
            jnp.sum(weight * part[:, (q + 1) * mine : (q + 2) * mine], axis=0) / bottom
            for q in range(2)
        ]
    ).reshape(2, mine * BLK)

    own_r = join(lax.dynamic_slice_in_dim(r, chip * mine, mine, 1))
    own_log = lax.dynamic_slice_in_dim(source_log, chip * mine, mine)
    x_half = 0.5 * jnp.sum(jnp.square(source_latent.astype(f32)), axis=0)
    out_source = (bias_of(own_log, own_r).reshape(-1) + x_half) / 32.0
    b = bias_of(target_log, join_pair(c, d))
    out_target = lax.dynamic_slice_in_dim((b - minus_half) / 32.0, core * own_k, own_k).reshape(-1)
    return out_source, out_target, mapped


def solution(mesh):
    in_specs = (
        P(None, ("row", "col")),
        P(None, "col"),
        P("row"),
        P("col"),
        P(None, "col"),
        P("row", None),
    )
    out_specs = (P(("row", "col")), P("col"), P(None, ("row", "col")))
    return jax.shard_map(
        on_device, mesh=mesh, in_specs=in_specs, out_specs=out_specs, check_vma=False
    )
```

```python
import functools

import jax
import jax.numpy as jnp
from jax import lax
from jax.experimental import pallas as pl
from jax.experimental.pallas import tpu as pltpu
from jax.sharding import PartitionSpec as P

LAT = 64
BLK = 128
NEG = -1e30
LN2 = 0.6931471805599453
KAPPA = 0.3125 / LN2
LONG_TURN = 64
SHORT_TURN = 32
PACK = 80
GROUP = 16


def chip_groups(cols):
    return [[c for c in range(cols) if c % 2 == core] for core in range(2)]


def swap_cores(x, cols):
    return lax.ppermute(x, "col", [(i, i ^ 1) for i in range(cols)])


def exchange(x, axis, groups=None):
    return lax.all_to_all(x, axis, 0, 0, axis_index_groups=groups)


def join(parts):
    top = jnp.max(parts, axis=0)
    return top + jnp.log2(jnp.sum(jnp.exp2(parts - top[None]), axis=0))


def join_pair(a, b):
    return jnp.maximum(a, b) + jnp.log2(1.0 + jnp.exp2(-jnp.abs(a - b)))


def bias_of(mass, level):
    return 3.2 * (mass - LN2 * level)


def pieces(a):
    hi = a.astype(jnp.bfloat16)
    rest = a - hi.astype(jnp.float32)
    mid = rest.astype(jnp.bfloat16)
    low = (rest - mid.astype(jnp.float32)).astype(jnp.bfloat16)
    return hi, mid, low


def fill_hot(hot_ref):
    row = lax.broadcasted_iota(jnp.int32, hot_ref.shape[1:], 0)
    for q in range(GROUP):
        hot_ref[q] = jnp.where((row & (GROUP - 1)) == q, 1.0, 0.0).astype(jnp.bfloat16)


def fill_biased(plain_ref, bias, full_ref):
    for first in range(0, plain_ref.shape[0], GROUP):
        hi, mid, low = pieces(bias[first : first + GROUP])
        blank = jnp.zeros((LAT, BLK), jnp.bfloat16)
        side = jnp.concatenate([blank, hi, mid, low, jnp.ones_like(hi)], axis=0).T
        for block in range(first, first + GROUP):
            full_ref[block] = plain_ref[block] + side


def fill_tails(bias, tail_ref):
    row = lax.broadcasted_iota(jnp.int32, (GROUP, BLK), 0)
    hi, mid, low = (p.astype(jnp.float32) for p in pieces(bias))
    for block in range(bias.shape[0]):
        one = slice(block, block + 1)
        rows = jnp.where(row == 1, mid[one], jnp.where(row == 2, low[one], 0.0))
        tail_ref[block] = jnp.where(row == 0, hi[one], rows).astype(jnp.bfloat16)


def columns(jb):
    return pl.ds(pl.multiple_of(jb * BLK, BLK), BLK)


def dot(lhs, rhs):
    return jnp.dot(lhs, rhs, preferred_element_type=jnp.float32)


def sweep(list_ref, body):
    count = list_ref[list_ref.shape[0] - 1, 0]
    long_turns = count // LONG_TURN
    left = count - long_turns * LONG_TURN

    def turn(first, size):
        row, start = first // BLK, first % BLK
        body([list_ref[row, start + u] for u in range(size)])

    def long_turn(g, c):
        turn(g * LONG_TURN, LONG_TURN)
        return c

    def short_turn(g, c):
        turn(long_turns * LONG_TURN + g * SHORT_TURN, SHORT_TURN)
        return c

    lax.fori_loop(0, long_turns, long_turn, 0)
    lax.fori_loop(0, (left + (SHORT_TURN - 1)) // SHORT_TURN, short_turn, 0)


def source_of(e):
    return e >> 6


def target_of(e):
    return e & 63


def fold_into(index, m, s, m_ref, s_ref):
    old = m_ref[index]
    new = jnp.maximum(old, m)
    s_ref[index] = s_ref[index] * jnp.exp2((old - new) * KAPPA) + s * jnp.exp2((m - new) * KAPPA)
    m_ref[index] = new


def finish(m, s):
    top = jnp.max(m, axis=1)
    total = jnp.sum(s * jnp.exp2((m - top[:, None, :]) * KAPPA), axis=1)
    return jnp.where(total > 0.0, top * KAPPA + jnp.log2(total), NEG)


def partial_stats(acc):
    split = acc.reshape(BLK // 8, 8, BLK)
    m = jnp.max(split, axis=0)
    return m, jnp.sum(jnp.exp2((split - m[None]) * KAPPA), axis=0)


def clear(m_ref, s_ref):
    m_ref[...] = jnp.full_like(m_ref, NEG)
    s_ref[...] = jnp.zeros_like(s_ref)


def source_block(x_ref, s):
    return x_ref[s >> 1, :, columns(s & 1)]


def no_tail(index):
    return jnp.zeros((GROUP, BLK), jnp.bfloat16)


def target_by_source(entries, x_ref, yt_ref, hot_ref, tail=no_tail):
    accs = []
    for e in entries:
        source = jnp.minimum(source_of(e), 2 * x_ref.shape[0] - 1)
        parts = [source_block(x_ref, source), hot_ref[e & (GROUP - 1)], tail(source)]
        accs.append(dot(yt_ref[target_of(e) & 31], jnp.concatenate(parts, axis=0)))
    return accs


def source_by_target(entries, pack_ref, xt_ref, hot_ref, tail=no_tail):
    accs = []
    for e in entries:
        source, target = jnp.minimum(source_of(e), xt_ref.shape[0] - 1), target_of(e) & 31
        block = pack_ref[:LAT, columns(target)]
        parts = [block, hot_ref[source & (GROUP - 1)], tail(target)]
        accs.append(dot(xt_ref[source], jnp.concatenate(parts, axis=0)))
    return accs


def plain_sum(acc):
    return jnp.sum(jnp.exp2(acc * KAPPA).reshape(BLK // 8, 8, BLK), axis=0)


def total(s_ref):
    return jnp.sum(s_ref[: s_ref.shape[0] - 1], axis=1)


def transposed(block):
    return jnp.concatenate([block, jnp.zeros_like(block)], axis=0).T


def target_side_kernel(pack_ref, yt0_ref, minus_half_ref):
    for q in range(yt0_ref.shape[0]):
        block = pack_ref[:LAT, q * BLK : (q + 1) * BLK]
        yt0_ref[q] = transposed(block)
        minus_half_ref[q : q + 1, :] = -0.5 * jnp.sum(
            jnp.square(block.astype(jnp.float32)), axis=0, keepdims=True
        )


def spread_kernel(in_ref, out_ref):
    out_ref[...] = jnp.broadcast_to(in_ref[...][None], out_ref.shape)


def source_side_kernel(x_ref, xt0_ref):
    for q in range(xt0_ref.shape[0]):
        xt0_ref[q] = transposed(x_ref[q // 2, :, (q % 2) * BLK : (q % 2 + 1) * BLK])


def start_copy(from_ref, to_ref, sem):
    copy = pltpu.make_async_copy(from_ref, to_ref, sem)
    copy.start()
    return copy


def first_row_kernel(
    tiles_ref, b_ref, x_ref, yt0_ref, out_ref, list_ref, side_ref, sems, yt_ref, hot_ref, m_ref, s_ref
):
    copy = start_copy(tiles_ref, list_ref, sems.at[0])
    fill_hot(hot_ref)
    clear(m_ref, s_ref)
    fill_biased(yt0_ref, b_ref[...], yt_ref)
    copy.wait()

    def body(entries):
        stats = [partial_stats(a) for a in target_by_source(entries, x_ref, yt_ref, hot_ref)]
        for e, (m, s) in zip(entries, stats):
            fold_into(source_of(e), m, s, m_ref, s_ref)

    sweep(list_ref, body)
    n = m_ref.shape[0] - 1
    out_ref[...] = jnp.broadcast_to(finish(m_ref[:n], s_ref[:n])[None], out_ref.shape)


def first_col_kernel(
    tiles_ref, log_ref, xt0_ref, pack_ref, r_ref, out_ref, a_ref, next_ref, list_ref, side_ref, sems, xt_ref, hot_ref, m_ref, s_ref
):
    mass = start_copy(log_ref, side_ref.at[0], sems.at[1])
    copy = start_copy(tiles_ref, list_ref, sems.at[0])
    fill_hot(hot_ref)
    clear(m_ref, s_ref)
    level = join(r_ref[...])
    mass.wait()
    a = bias_of(side_ref[0], level)
    side_ref[1] = a
    side_ref[2] = a + 3.2 * side_ref[0]
    out_a = start_copy(side_ref.at[1], a_ref, sems.at[2])
    out_next = start_copy(side_ref.at[2], next_ref, sems.at[3])
    fill_biased(xt0_ref, a, xt_ref)
    copy.wait()

    def body(entries):
        stats = [partial_stats(a) for a in source_by_target(entries, pack_ref, xt_ref, hot_ref)]
        for e, (m, s) in zip(entries, stats):
            fold_into(target_of(e), m, s, m_ref, s_ref)

    sweep(list_ref, body)
    k = m_ref.shape[0] - 1
    out_ref[...] = jnp.broadcast_to(finish(m_ref[:k], s_ref[:k])[None], out_ref.shape)
    out_a.wait()
    out_next.wait()


def row_kernel(
    tiles_ref, log_ref, a_ref, x_ref, yt0_ref, c_ref, d_ref, out_ref, b_ref, next_ref, list_ref, side_ref, sems, yt_ref, hot_ref, tail_ref, s_ref
):
    mass = start_copy(log_ref, side_ref.at[0], sems.at[1])
    in_a = start_copy(a_ref, side_ref.at[3], sems.at[4])
    copy = start_copy(tiles_ref, list_ref, sems.at[0])
    fill_hot(hot_ref)
    s_ref[...] = jnp.zeros_like(s_ref)
    level = join_pair(c_ref[...], d_ref[...])
    mass.wait()
    b = bias_of(side_ref[0], level)
    side_ref[1] = b
    side_ref[2] = b + 3.2 * side_ref[0]
    out_b = start_copy(side_ref.at[1], b_ref, sems.at[2])
    out_next = start_copy(side_ref.at[2], next_ref, sems.at[3])
    fill_biased(yt0_ref, b, yt_ref)
    in_a.wait()
    fill_tails(side_ref[3], tail_ref)
    copy.wait()

    def body(entries):
        accs = target_by_source(entries, x_ref, yt_ref, hot_ref, lambda q: tail_ref[q])
        for e, s in zip(entries, [plain_sum(acc) for acc in accs]):
            s_ref[source_of(e)] += s

    sweep(list_ref, body)
    out_ref[...] = jnp.broadcast_to(total(s_ref)[None], out_ref.shape)
    out_b.wait()
    out_next.wait()


def col_kernel(
    tiles_ref, lifted_ref, b_ref, xt0_ref, pack_ref, r_ref, out_ref, a_ref, list_ref, side_ref, sems, xt_ref, hot_ref, tail_ref, s_ref
):
    lifted = start_copy(lifted_ref, side_ref.at[0], sems.at[1])
    in_b = start_copy(b_ref, side_ref.at[3], sems.at[4])
    copy = start_copy(tiles_ref, list_ref, sems.at[0])
    fill_hot(hot_ref)
    s_ref[...] = jnp.zeros_like(s_ref)
    drop = 3.2 * jnp.log(jnp.sum(r_ref[...], axis=0))
    lifted.wait()
    a = side_ref[0] - drop
    side_ref[1] = a
    out_a = start_copy(side_ref.at[1], a_ref, sems.at[2])
    fill_biased(xt0_ref, a, xt_ref)
    in_b.wait()
    fill_tails(side_ref[3], tail_ref)
    copy.wait()

    def body(entries):
        accs = source_by_target(entries, pack_ref, xt_ref, hot_ref, lambda q: tail_ref[q])
        for e, s in zip(entries, [plain_sum(acc) for acc in accs]):
            s_ref[target_of(e)] += s

    sweep(list_ref, body)
    out_ref[...] = jnp.broadcast_to(total(s_ref)[None], out_ref.shape)
    out_a.wait()


def project_kernel(
    tiles_ref, lifted_ref, a_ref, x_ref, yt0_ref, pack_ref, c_ref, d_ref, out_ref, b_ref, list_ref, side_ref, sems, yt_ref, hot_ref, tail_ref, w_ref
):
    lifted = start_copy(lifted_ref, side_ref.at[0], sems.at[1])
    in_a = start_copy(a_ref, side_ref.at[3], sems.at[4])
    copy = start_copy(tiles_ref, list_ref, sems.at[0])
    fill_hot(hot_ref)
    w_ref[...] = jnp.zeros_like(w_ref)
    drop = 3.2 * jnp.log(c_ref[...] + d_ref[...])
    lifted.wait()
    b = side_ref[0] - drop
    side_ref[1] = b
    out_b = start_copy(side_ref.at[1], b_ref, sems.at[2])
    fill_biased(yt0_ref, b, yt_ref)
    in_a.wait()
    fill_tails(side_ref[3], tail_ref)
    copy.wait()

    def body(entries):
        weighted = []
        accs = target_by_source(entries, x_ref, yt_ref, hot_ref, lambda q: tail_ref[q])
        for e, acc in zip(entries, accs):
            p = jnp.exp2(acc * KAPPA)
            hi = p.astype(jnp.bfloat16)
            low = (p - hi.astype(jnp.float32)).astype(jnp.bfloat16)
            side = pack_ref[LAT:, columns(target_of(e) & 31)]
            both = jnp.concatenate([hi, low], axis=0)
            weighted.append(dot(jnp.concatenate([side, side], axis=1), both)[:8])
        for e, w in zip(entries, weighted):
            w_ref[source_of(e)] += w

    sweep(list_ref, body)
    out_ref[...] = jnp.zeros_like(out_ref)
    for ib in range(2 * x_ref.shape[0]):
        w = w_ref[ib]
        for place, row in enumerate((2, 0, 1)):
            first = 2 * place + ib % 2
            out_ref[ib // 2, first : first + 1, :] = w[row : row + 1]
    out_b.wait()


VMEM = pl.BlockSpec(memory_space=pltpu.VMEM)
HBM = pl.BlockSpec(memory_space=pltpu.HBM)


def call(kernel, outs, scratch, far, near, far_outs=0):
    put = pltpu.with_memory_space_constraint
    return pl.pallas_call(
        kernel,
        out_shape=outs,
        in_specs=[HBM] * len(far) + [VMEM] * len(near),
        out_specs=[VMEM] * (len(outs) - far_outs) + [HBM] * far_outs,
        scratch_shapes=scratch,
        compiler_params=pltpu.CompilerParams(vmem_limit_bytes=16 << 20),
    )(*(put(a, pltpu.HBM) for a in far), *(put(a, pltpu.VMEM) for a in near))


def tile_list(support, chip, per_chip, slots):
    rows, per_list = support.shape
    owned = support // per_chip == chip
    flags = owned.astype(jnp.float32)
    upto = (jnp.arange(per_list)[:, None] <= jnp.arange(per_list)[None, :]).astype(jnp.float32)
    before = (jnp.arange(rows)[None, :] < jnp.arange(rows)[:, None]).astype(jnp.float32)
    within = flags @ upto
    start = before @ within[:, -1:]
    place = jnp.where(owned, (within + start).astype(jnp.int32) - 1, -1)
    count = jnp.sum(owned.astype(jnp.int32))
    code = jnp.arange(rows, dtype=jnp.int32)[:, None] * 64 + support % per_chip
    slot = jnp.arange(slots, dtype=jnp.int32)
    listed = jnp.sum(
        jnp.where(place[:, :, None] == slot, code[:, :, None], 0), axis=(0, 1), dtype=jnp.int32
    )
    listed = jnp.where(slot < count, listed, rows * 64 + per_chip)
    return jnp.concatenate([listed, jnp.broadcast_to(count, (BLK,))]).reshape(-1, BLK)


def on_device(
    source_latent, target_latent, log_source_mass, log_target_mass, target_coords, support
):
    rows, cols = lax.axis_size("row"), lax.axis_size("col")
    here = lax.axis_index("col")
    chip, core = here // 2, here % 2
    chips = cols // 2
    mine = support.shape[0] // cols
    own_k = target_latent.shape[1] // BLK
    n, k = chips * mine, 2 * own_k
    bf16, f32 = jnp.bfloat16, jnp.float32
    by_chip = chip_groups(cols)

    def of_core(a):
        split = a.reshape((chips, 2, mine) + a.shape[1:])
        split = jnp.where(core == 0, split[:, 0], split[:, 1])
        return split.reshape((n,) + a.shape[1:])

    spread = pl.pallas_call(
        spread_kernel,
        out_shape=jax.ShapeDtypeStruct((chips,) + source_latent.shape, bf16),
        in_specs=[VMEM],
        out_specs=VMEM,
    )(source_latent)
    spread, support = lax.optimization_barrier((spread, support))
    x = exchange(spread, "col", by_chip)
    tiles = tile_list(of_core(support), chip, k, 12 * mine * chips)
    tiles, target_latent, target_coords, log_target_mass = lax.optimization_barrier(
        (tiles, target_latent, target_coords, log_target_mass)
    )

    def pair(a):
        other = swap_cores(a, cols)
        return jnp.concatenate(
            [jnp.where(core == 0, a, other), jnp.where(core == 0, other, a)], axis=1
        )

    width = 2 * target_latent.shape[1]
    targets = pair(target_latent)
    coords, target_log = pair(target_coords), pair(log_target_mass[None])
    pack = jnp.concatenate(
        [targets, coords, jnp.ones((1, width), bf16), jnp.zeros((PACK - LAT - 3, width), bf16)],
        axis=0,
    )
    target_log = target_log.astype(f32).reshape(k, BLK)
    source_log = of_core(log_source_mass.reshape(-1, BLK))

    common = [
        pltpu.SMEM(tiles.shape, jnp.int32),
        pltpu.VMEM((4, n, BLK), f32),
        pltpu.SemaphoreType.DMA((5,)),
        pltpu.VMEM((n, BLK, BLK), bf16),
        pltpu.VMEM((GROUP, 3 * GROUP, BLK), bf16),
    ]
    sums = pltpu.VMEM((n + 1, 8, BLK), f32)
    first_scratch = common + [sums, sums]
    scratch = common + [pltpu.VMEM((n, GROUP, BLK), bf16), sums]

    tiles, source_log, target_log = lax.optimization_barrier((tiles, source_log, target_log))
    turned = pltpu.VMEM((n, BLK, BLK), bf16)
    yt0, minus_half = call(
        target_side_kernel, [turned, pltpu.VMEM((k, BLK), f32)], [], [], [pack]
    )
    small = pltpu.HBM((n, BLK), f32)
    to_chips = jax.ShapeDtypeStruct((chips, n, BLK), f32)
    to_rows = jax.ShapeDtypeStruct((rows, k, BLK), f32)
    to_owners = jax.ShapeDtypeStruct((chips, 8, BLK), f32)

    (r,) = call(first_row_kernel, [to_chips], first_scratch, [tiles], [minus_half, x, yt0])
    (xt0,) = call(source_side_kernel, [turned], [], [], [x])
    r = exchange(r, "col", by_chip)
    c, a, lifted = call(
        first_col_kernel,
        [to_rows, small, small],
        first_scratch,
        [tiles, source_log],
        [xt0, pack, r],
        2,
    )
    c = join(exchange(c, "row"))
    d = swap_cores(c, cols)
    r, b, target_lifted = call(
        row_kernel, [to_chips, small, small], scratch, [tiles, target_log, a], [x, yt0, c, d], 2
    )
    r = exchange(r, "col", by_chip)
    c, a = call(
        col_kernel, [to_rows, small], scratch, [tiles, lifted, b], [xt0, pack, r], 1
    )
    c = jnp.sum(exchange(c, "row"), axis=0)
    d = swap_cores(c, cols)
    part, b = call(
        project_kernel,
        [to_owners, small],
        scratch,
        [tiles, target_lifted, a],
        [x, yt0, pack, c, d],
        1,
    )
    part, a, b, source_latent = lax.optimization_barrier((part, a, b, source_latent))
    part = jnp.sum(exchange(part, "col", by_chip), axis=0)
    mapped = part[mine : 3 * mine].reshape(2, mine, BLK) / part[:mine]
    mapped = mapped.reshape(2, mine * BLK)

    own_a = lax.dynamic_slice_in_dim(a, chip * mine, mine).reshape(-1)
    x_half = 0.5 * jnp.sum(jnp.square(source_latent.astype(f32)), axis=0)
    out_source = (own_a + x_half) / 32.0
    out_target = lax.dynamic_slice_in_dim((b - minus_half) / 32.0, core * own_k, own_k).reshape(-1)
    return out_source, out_target, mapped


def solution(mesh):
    in_specs = (
        P(None, ("row", "col")),
        P(None, "col"),
        P("row"),
        P("col"),
        P(None, "col"),
        P("row", None),
    )
    out_specs = (P(("row", "col")), P("col"), P(None, ("row", "col")))
    return jax.shard_map(
        on_device, mesh=mesh, in_specs=in_specs, out_specs=out_specs, check_vma=False
    )
```

```python
import functools

import jax
import jax.numpy as jnp
from jax import lax
from jax.experimental import pallas as pl
from jax.experimental.pallas import tpu as pltpu
from jax.sharding import PartitionSpec as P

LAT = 64
BLK = 128
NEG = -1e30
LN2 = 0.6931471805599453
KAPPA = 0.3125 / LN2
TURNS = (64, 32, 16)
PACK = 80
GROUP = 16
PAD = 32 * 64 + 32


def chip_groups(cols):
    return [[c for c in range(cols) if c % 2 == core] for core in range(2)]


def swap_cores(x, cols):
    return lax.ppermute(x, "col", [(i, i ^ 1) for i in range(cols)])


def exchange(x, axis, groups=None):
    return lax.all_to_all(x, axis, 0, 0, axis_index_groups=groups)


def join(parts):
    top = jnp.max(parts, axis=0)
    return top + jnp.log2(jnp.sum(jnp.exp2(parts - top[None]), axis=0))


def join_pair(a, b):
    top = jnp.maximum(jnp.max(a, axis=0), jnp.max(b, axis=0))
    total = jnp.sum(jnp.exp2(a - top[None]), axis=0) + jnp.sum(jnp.exp2(b - top[None]), axis=0)
    return top + jnp.log2(total)


def bias_of(level):
    return -3.2 * LN2 * level


def pieces(a):
    hi = a.astype(jnp.bfloat16)
    rest = a - hi.astype(jnp.float32)
    mid = rest.astype(jnp.bfloat16)
    low = (rest - mid.astype(jnp.float32)).astype(jnp.bfloat16)
    return hi, mid, low


def fill_hot(hot_ref):
    row = lax.broadcasted_iota(jnp.int32, hot_ref.shape[1:], 0)
    for q in range(GROUP):
        hot_ref[q] = jnp.where((row & (GROUP - 1)) == q, 1.0, 0.0).astype(jnp.bfloat16)


def fill_biased(plain_ref, bias, full_ref):
    for first in range(0, plain_ref.shape[0], GROUP):
        hi, mid, low = pieces(bias[first : first + GROUP])
        blank = jnp.zeros((LAT, BLK), jnp.bfloat16)
        side = jnp.concatenate([blank, hi, mid, low, jnp.ones_like(hi)], axis=0).T
        for block in range(first, first + GROUP):
            full_ref[block] = plain_ref[block] + side


def fill_tails(bias, tail_ref):
    row = lax.broadcasted_iota(jnp.int32, (GROUP, BLK), 0)
    hi, mid, low = (p.astype(jnp.float32) for p in pieces(bias))
    for block in range(bias.shape[0]):
        one = slice(block, block + 1)
        rows = jnp.where(row == 1, mid[one], jnp.where(row == 2, low[one], 0.0))
        tail_ref[block] = jnp.where(row == 0, hi[one], rows).astype(jnp.bfloat16)


def columns(jb):
    return pl.ds(pl.multiple_of(jb * BLK, BLK), BLK)


def dot(lhs, rhs):
    return jnp.dot(lhs, rhs, preferred_element_type=jnp.float32)


def sweep(list_ref, body):
    count = list_ref[list_ref.shape[0] - 1, 0]
    done = 0
    for size in TURNS:
        left = jnp.maximum(count - done, 0)
        turns = (left + (size // 2 if size > TURNS[-1] else size - 1)) // size

        def turn(g, c, size=size, done=done):
            first = done + g * size
            row, start = first // BLK, first % BLK
            body([list_ref[row, start + u] + PAD for u in range(size)])
            return c

        lax.fori_loop(0, turns, turn, 0)
        done = done + turns * size


def source_of(e):
    return e >> 6


def target_of(e):
    return e & 63


def fold_into(index, m, s, m_ref, s_ref):
    old = m_ref[index]
    new = jnp.maximum(old, m)
    s_ref[index] = s_ref[index] * jnp.exp2((old - new) * KAPPA) + s * jnp.exp2((m - new) * KAPPA)
    m_ref[index] = new


def finish(m, s):
    top = jnp.max(m, axis=1)
    total = jnp.sum(s * jnp.exp2((m - top[:, None, :]) * KAPPA), axis=1)
    return jnp.where(total > 0.0, top * KAPPA + jnp.log2(total), NEG)


def partial_stats(acc):
    split = acc.reshape(BLK // 8, 8, BLK)
    m = jnp.max(split, axis=0)
    return m, jnp.sum(jnp.exp2((split - m[None]) * KAPPA), axis=0)


def clear(m_ref, s_ref):
    m_ref[...] = jnp.full_like(m_ref, NEG)
    s_ref[...] = jnp.zeros_like(s_ref)


def source_block(x_ref, s):
    return x_ref[s >> 1, :, columns(s & 1)]


def no_tail(index):
    return jnp.zeros((GROUP, BLK), jnp.bfloat16)


def target_by_source(entries, x_ref, yt_ref, hot_ref, tail=no_tail):
    accs = []
    for e in entries:
        source = jnp.minimum(source_of(e), 2 * x_ref.shape[0] - 1)
        parts = [source_block(x_ref, source), hot_ref[e & (GROUP - 1)], tail(source)]
        accs.append(dot(yt_ref[target_of(e) & 31], jnp.concatenate(parts, axis=0)))
    return accs


def source_by_target(entries, pack_ref, xt_ref, hot_ref, tail=no_tail):
    accs = []
    for e in entries:
        source, target = jnp.minimum(source_of(e), xt_ref.shape[0] - 1), target_of(e) & 31
        block = pack_ref[:LAT, columns(target)]
        parts = [block, hot_ref[source & (GROUP - 1)], tail(target)]
        accs.append(dot(xt_ref[source], jnp.concatenate(parts, axis=0)))
    return accs


def plain_sum(acc):
    return jnp.sum(jnp.exp2(acc * KAPPA).reshape(BLK // 8, 8, BLK), axis=0)


def finish_plain(s_ref, bias):
    total = jnp.sum(s_ref[: s_ref.shape[0] - 1], axis=1)
    live = total > 0.0
    return jnp.where(live, jnp.log2(jnp.where(live, total, 1.0)), NEG) - KAPPA * bias


def put_level(level, mass, out_ref):
    out_ref[...] = jnp.broadcast_to((level - mass * (1.0 / LN2))[None], out_ref.shape)


def transposed(block):
    return jnp.concatenate([block, jnp.zeros_like(block)], axis=0).T


def target_side_kernel(pack_ref, yt0_ref, minus_half_ref, hot_ref):
    fill_hot(hot_ref)
    for q in range(yt0_ref.shape[0]):
        block = pack_ref[:LAT, q * BLK : (q + 1) * BLK]
        yt0_ref[q] = transposed(block)
        minus_half_ref[q : q + 1, :] = -0.5 * jnp.sum(
            jnp.square(block.astype(jnp.float32)), axis=0, keepdims=True
        )


def spread_kernel(in_ref, out_ref):
    out_ref[...] = jnp.broadcast_to(in_ref[...][None], out_ref.shape)


def start_copy(from_ref, to_ref, sem):
    copy = pltpu.make_async_copy(from_ref, to_ref, sem)
    copy.start()
    return copy


def first_row_kernel(
    tiles_ref, log_ref, b_ref, hot_ref, x_ref, yt0_ref, out_ref, xt0_ref, list_ref, side_ref, sems, yt_ref, m_ref, s_ref
):
    copy = start_copy(tiles_ref, list_ref, sems.at[0])
    mass = start_copy(log_ref, side_ref.at[0], sems.at[1])
    clear(m_ref, s_ref)
    fill_biased(yt0_ref, b_ref[...], yt_ref)
    for q in range(xt0_ref.shape[0]):
        xt0_ref[q] = transposed(x_ref[q // 2, :, (q % 2) * BLK : (q % 2 + 1) * BLK])
    copy.wait()

    def body(entries):
        stats = [partial_stats(a) for a in target_by_source(entries, x_ref, yt_ref, hot_ref)]
        for e, (m, s) in zip(entries, stats):
            fold_into(source_of(e), m, s, m_ref, s_ref)

    sweep(list_ref, body)
    n = m_ref.shape[0] - 1
    mass.wait()
    put_level(finish(m_ref[:n], s_ref[:n]), side_ref[0], out_ref)


def first_col_kernel(
    tiles_ref, log_ref, hot_ref, xt0_ref, pack_ref, r_ref, out_ref, tail_out_ref, a_ref, list_ref, side_ref, sems, xt_ref, m_ref, s_ref
):
    copy = start_copy(tiles_ref, list_ref, sems.at[0])
    mass = start_copy(log_ref, side_ref.at[0], sems.at[1])
    a = bias_of(join(r_ref[...]))
    side_ref[1] = a
    out_a = start_copy(side_ref.at[1], a_ref, sems.at[2])
    clear(m_ref, s_ref)
    fill_biased(xt0_ref, a, xt_ref)
    fill_tails(a, tail_out_ref)
    copy.wait()

    def body(entries):
        stats = [partial_stats(a) for a in source_by_target(entries, pack_ref, xt_ref, hot_ref)]
        for e, (m, s) in zip(entries, stats):
            fold_into(target_of(e), m, s, m_ref, s_ref)

    sweep(list_ref, body)
    k = m_ref.shape[0] - 1
    mass.wait()
    put_level(finish(m_ref[:k], s_ref[:k]), side_ref[0], out_ref)
    out_a.wait()


def row_kernel(
    tiles_ref, log_ref, a_ref, hot_ref, tail_ref, x_ref, yt0_ref, c_ref, d_ref, out_ref, tail_out_ref, b_ref, list_ref, side_ref, sems, yt_ref, s_ref
):
    copy = start_copy(tiles_ref, list_ref, sems.at[0])
    mass = start_copy(log_ref, side_ref.at[0], sems.at[1])
    in_a = start_copy(a_ref, side_ref.at[2], sems.at[3])
    b = bias_of(join_pair(c_ref[...], d_ref[...]))
    side_ref[1] = b
    out_b = start_copy(side_ref.at[1], b_ref, sems.at[2])
    s_ref[...] = jnp.zeros_like(s_ref)
    fill_biased(yt0_ref, b, yt_ref)
    fill_tails(b, tail_out_ref)
    copy.wait()

    def body(entries):
        accs = target_by_source(entries, x_ref, yt_ref, hot_ref, lambda q: tail_ref[q])
        for e, s in zip(entries, [plain_sum(acc) for acc in accs]):
            s_ref[source_of(e)] += s

    sweep(list_ref, body)
    mass.wait()
    in_a.wait()
    put_level(finish_plain(s_ref, side_ref[2]), side_ref[0], out_ref)
    out_b.wait()


def col_kernel(
    tiles_ref, log_ref, b_ref, hot_ref, tail_ref, xt0_ref, pack_ref, r_ref, out_ref, tail_out_ref, a_ref, list_ref, side_ref, sems, xt_ref, s_ref
):
    copy = start_copy(tiles_ref, list_ref, sems.at[0])
    mass = start_copy(log_ref, side_ref.at[0], sems.at[1])
    in_b = start_copy(b_ref, side_ref.at[2], sems.at[3])
    a = bias_of(join(r_ref[...]))
    side_ref[1] = a
    out_a = start_copy(side_ref.at[1], a_ref, sems.at[2])
    s_ref[...] = jnp.zeros_like(s_ref)
    fill_biased(xt0_ref, a, xt_ref)
    fill_tails(a, tail_out_ref)
    copy.wait()

    def body(entries):
        accs = source_by_target(entries, pack_ref, xt_ref, hot_ref, lambda q: tail_ref[q])
        for e, s in zip(entries, [plain_sum(acc) for acc in accs]):
            s_ref[target_of(e)] += s

    sweep(list_ref, body)
    mass.wait()
    in_b.wait()
    put_level(finish_plain(s_ref, side_ref[2]), side_ref[0], out_ref)
    out_a.wait()


def project_kernel(
    tiles_ref, hot_ref, tail_ref, x_ref, yt0_ref, pack_ref, c_ref, d_ref, out_ref, b_ref, list_ref, side_ref, sems, yt_ref, w_ref
):
    copy = start_copy(tiles_ref, list_ref, sems.at[0])
    b = bias_of(join_pair(c_ref[...], d_ref[...]))
    side_ref[1] = b
    out_b = start_copy(side_ref.at[1], b_ref, sems.at[2])
    w_ref[...] = jnp.zeros_like(w_ref)
    fill_biased(yt0_ref, b, yt_ref)
    copy.wait()

    def body(entries):
        weighted = []
        accs = target_by_source(entries, x_ref, yt_ref, hot_ref, lambda q: tail_ref[q])
        for e, acc in zip(entries, accs):
            p = jnp.exp2(acc * KAPPA)
            hi = p.astype(jnp.bfloat16)
            low = (p - hi.astype(jnp.float32)).astype(jnp.bfloat16)
            side = pack_ref[LAT:, columns(target_of(e) & 31)]
            both = jnp.concatenate([hi, low], axis=0)
            weighted.append(dot(jnp.concatenate([side, side], axis=1), both)[:8])
        for e, w in zip(entries, weighted):
            w_ref[source_of(e)] += w

    sweep(list_ref, body)
    out_ref[...] = jnp.zeros_like(out_ref)
    for ib in range(2 * x_ref.shape[0]):
        w = w_ref[ib]
        for place, row in enumerate((2, 0, 1)):
            first = 2 * place + ib % 2
            out_ref[ib // 2, first : first + 1, :] = w[row : row + 1]
    out_b.wait()


VMEM = pl.BlockSpec(memory_space=pltpu.VMEM)
HBM = pl.BlockSpec(memory_space=pltpu.HBM)


def call(kernel, outs, scratch, far, near, far_outs=0):
    put = pltpu.with_memory_space_constraint
    return pl.pallas_call(
        kernel,
        out_shape=outs,
        in_specs=[HBM] * len(far) + [VMEM] * len(near),
        out_specs=[VMEM] * (len(outs) - far_outs) + [HBM] * far_outs,
        scratch_shapes=scratch,
        compiler_params=pltpu.CompilerParams(vmem_limit_bytes=16 << 20),
    )(*(put(a, pltpu.HBM) for a in far), *(put(a, pltpu.VMEM) for a in near))


def tile_list(support, chip, core, per_chip, slots):
    rows, per_list = support.shape
    row = jnp.arange(rows, dtype=jnp.int32)[:, None]
    owned = (support // per_chip == chip) & (row // 2 % 2 == core)
    flags = owned.astype(jnp.float32)
    upto = (jnp.arange(per_list)[:, None] <= jnp.arange(per_list)[None, :]).astype(jnp.float32)
    before = (jnp.arange(rows)[None, :] < jnp.arange(rows)[:, None]).astype(jnp.float32)
    within = flags @ upto
    start = before @ within[:, -1:]
    place = jnp.where(owned, (within + start).astype(jnp.int32) - 1, -1)
    code = (row // 4 * 2 + row % 2) * 64 + support % per_chip - PAD
    slot = jnp.arange(slots + BLK, dtype=jnp.int32).reshape(-1, BLK)
    place, code = place[:, :, None, None], code[:, :, None, None]
    last = jnp.where((slot >= slots) & (place >= 0), 1, 0)
    listed = jnp.where(place == slot, code, last)
    return jnp.sum(listed, axis=(0, 1), dtype=jnp.int32), within


def on_device(
    source_latent, target_latent, log_source_mass, log_target_mass, target_coords, support
):
    rows, cols = lax.axis_size("row"), lax.axis_size("col")
    here = lax.axis_index("col")
    chip, core = here // 2, here % 2
    chips = cols // 2
    mine = support.shape[0] // cols
    own_k = target_latent.shape[1] // BLK
    n, k = chips * mine, 2 * own_k
    bf16, f32 = jnp.bfloat16, jnp.float32
    by_chip = chip_groups(cols)

    def of_core(a):
        split = a.reshape((chips, 2, mine) + a.shape[1:])
        split = jnp.where(core == 0, split[:, 0], split[:, 1])
        return split.reshape((n,) + a.shape[1:])

    spread = pl.pallas_call(
        spread_kernel,
        out_shape=jax.ShapeDtypeStruct((chips,) + source_latent.shape, bf16),
        in_specs=[VMEM],
        out_specs=VMEM,
    )(source_latent)
    spread, support = lax.optimization_barrier((spread, support))
    x = exchange(spread, "col", by_chip)
    tiles, early = tile_list(support, chip, core, k, 12 * mine * chips)
    early, target_latent, target_coords, log_target_mass = lax.optimization_barrier(
        (early, target_latent, target_coords, log_target_mass)
    )

    def pair(a):
        other = swap_cores(a, cols)
        return jnp.concatenate(
            [jnp.where(core == 0, a, other), jnp.where(core == 0, other, a)], axis=1
        )

    width = 2 * target_latent.shape[1]
    targets = pair(target_latent)
    coords, target_log = pair(target_coords), pair(log_target_mass[None])
    pack = jnp.concatenate(
        [targets, coords, jnp.ones((1, width), bf16), jnp.zeros((PACK - LAT - 3, width), bf16)],
        axis=0,
    )
    common = [
        pltpu.SMEM(tiles.shape, jnp.int32),
        pltpu.VMEM((3, n, BLK), f32),
        pltpu.SemaphoreType.DMA((4,)),
        pltpu.VMEM((n, BLK, BLK), bf16),
    ]
    sums = pltpu.VMEM((n + 1, 8, BLK), f32)
    first_scratch = common + [sums, sums]
    scratch = common + [sums]

    target_log = target_log.astype(f32).reshape(k, BLK)
    source_log = of_core(log_source_mass.reshape(-1, BLK))
    tiles, source_log, target_log = lax.optimization_barrier((tiles, source_log, target_log))

    turned = pltpu.VMEM((n, BLK, BLK), bf16)
    hot_shape = pltpu.VMEM((GROUP, 3 * GROUP, BLK), bf16)
    yt0, minus_half, hot = call(
        target_side_kernel, [turned, pltpu.VMEM((k, BLK), f32), hot_shape], [], [], [pack]
    )
    tail_shape = pltpu.VMEM((n, GROUP, BLK), bf16)
    small = pltpu.HBM((n, BLK), f32)
    to_chips = jax.ShapeDtypeStruct((chips, n, BLK), f32)
    to_rows = jax.ShapeDtypeStruct((rows, k, BLK), f32)
    to_owners = jax.ShapeDtypeStruct((chips, 8, BLK), f32)
    by_sources, by_targets = [tiles, source_log], [tiles, target_log]

    r, xt0 = call(
        first_row_kernel,
        [to_chips, turned],
        first_scratch,
        by_sources,
        [minus_half, hot, x, yt0],
    )
    r = exchange(r, "col", by_chip)
    c, tail, a = call(
        first_col_kernel,
        [to_rows, tail_shape, small],
        first_scratch,
        by_targets,
        [hot, xt0, pack, r],
        1,
    )
    c = exchange(c, "row")
    d = swap_cores(c, cols)
    r, tail, b = call(
        row_kernel,
        [to_chips, tail_shape, small],
        scratch,
        by_sources + [a],
        [hot, tail, x, yt0, c, d],
        1,
    )
    r = exchange(r, "col", by_chip)
    c, tail, a = call(
        col_kernel,
        [to_rows, tail_shape, small],
        scratch,
        by_targets + [b],
        [hot, tail, xt0, pack, r],
        1,
    )
    c = exchange(c, "row")
    d = swap_cores(c, cols)
    part, b = call(
        project_kernel,
        [to_owners, small],
        scratch,
        [tiles],
        [hot, tail, x, yt0, pack, c, d],
        1,
    )
    part, a, b, source_latent = lax.optimization_barrier((part, a, b, source_latent))
    part = jnp.sum(exchange(part, "col", by_chip), axis=0)
    mapped = part[mine : 3 * mine].reshape(2, mine, BLK) / part[:mine]
    mapped = mapped.reshape(2, mine * BLK)

    own_a = lax.dynamic_slice_in_dim(a, chip * mine, mine).reshape(-1)
    x_half = 0.5 * jnp.sum(jnp.square(source_latent.astype(f32)), axis=0)
    out_source = (own_a + x_half) / 32.0
    out_target = lax.dynamic_slice_in_dim((b - minus_half) / 32.0, core * own_k, own_k).reshape(-1)
    return out_source, out_target, mapped


def solution(mesh):
    in_specs = (
        P(None, ("row", "col")),
        P(None, "col"),
        P("row"),
        P("col"),
        P(None, "col"),
        P("row", None),
    )
    out_specs = (P(("row", "col")), P("col"), P(None, ("row", "col")))
    return jax.shard_map(
        on_device, mesh=mesh, in_specs=in_specs, out_specs=out_specs, check_vma=False
    )
```

```python
import functools

import jax
import jax.numpy as jnp
from jax import lax
from jax.experimental import pallas as pl
from jax.experimental.pallas import tpu as pltpu
from jax.sharding import PartitionSpec as P

LAT = 64
BLK = 128
NEG = -1e30
LN2 = 0.6931471805599453
KAPPA = 0.3125 / LN2
PLAIN_TURNS = (128, 64, 32, 16)
TURNS = (64, 16)
PACK = 80
GROUP = 16
PAD = 32 * 64 + 32


def chip_groups(cols):
    return [[c for c in range(cols) if c % 2 == core] for core in range(2)]


def swap_cores(x, cols):
    return lax.ppermute(x, "col", [(i, i ^ 1) for i in range(cols)])


def exchange(x, axis, groups=None):
    return lax.all_to_all(x, axis, 0, 0, axis_index_groups=groups)


def join(parts):
    top = jnp.max(parts, axis=0)
    return top + jnp.log2(jnp.sum(jnp.exp2(parts - top[None]), axis=0))


def join_pair(a, b):
    top = jnp.maximum(jnp.max(a, axis=0), jnp.max(b, axis=0))
    total = jnp.sum(jnp.exp2(a - top[None]), axis=0) + jnp.sum(jnp.exp2(b - top[None]), axis=0)
    return top + jnp.log2(total)


def bias_of(level):
    return -3.2 * LN2 * level


def pieces(a):
    hi = a.astype(jnp.bfloat16)
    rest = a - hi.astype(jnp.float32)
    mid = rest.astype(jnp.bfloat16)
    low = (rest - mid.astype(jnp.float32)).astype(jnp.bfloat16)
    return hi, mid, low


def fill_hot(hot_ref):
    row = lax.broadcasted_iota(jnp.int32, hot_ref.shape[1:], 0)
    for q in range(GROUP):
        hot_ref[q] = jnp.where((row & (GROUP - 1)) == q, 1.0, 0.0).astype(jnp.bfloat16)


def fill_biased(plain_ref, bias, full_ref):
    for first in range(0, plain_ref.shape[0], GROUP):
        hi, mid, low = pieces(bias[first : first + GROUP])
        blank = jnp.zeros((LAT, BLK), jnp.bfloat16)
        side = jnp.concatenate([blank, hi, mid, low, jnp.ones_like(hi)], axis=0).T
        for block in range(first, first + GROUP):
            full_ref[block] = plain_ref[block] + side


def fill_tails(bias, tail_ref):
    row = lax.broadcasted_iota(jnp.int32, (GROUP, BLK), 0)
    hi, mid, low = (p.astype(jnp.float32) for p in pieces(bias))
    for block in range(bias.shape[0]):
        one = slice(block, block + 1)
        rows = jnp.where(row == 1, mid[one], jnp.where(row == 2, low[one], 0.0))
        tail_ref[block] = jnp.where(row == 0, hi[one], rows).astype(jnp.bfloat16)


def columns(jb):
    return pl.ds(pl.multiple_of(jb * BLK, BLK), BLK)


def dot(lhs, rhs):
    return jnp.dot(lhs, rhs, preferred_element_type=jnp.float32)


def sweep(list_ref, body, sizes=TURNS):
    count = list_ref[list_ref.shape[0] - 1, 0]
    done = 0
    for size in sizes:
        left = jnp.maximum(count - done, 0)
        turns = (left + (size // 4 if size > sizes[-1] else size) - 1) // size

        def turn(g, c, size=size, done=done):
            first = done + g * size
            row, start = first // BLK, first % BLK
            body([list_ref[row, start + u] + PAD for u in range(size)])
            return c

        lax.fori_loop(0, turns, turn, 0)
        done = done + turns * size


def source_of(e):
    return e >> 6


def target_of(e):
    return e & 63


def fold_into(index, m, s, m_ref, s_ref):
    old = m_ref[index]
    new = jnp.maximum(old, m)
    s_ref[index] = s_ref[index] * jnp.exp2((old - new) * KAPPA) + s * jnp.exp2((m - new) * KAPPA)
    m_ref[index] = new


def finish(m, s):
    top = jnp.max(m, axis=1)
    total = jnp.sum(s * jnp.exp2((m - top[:, None, :]) * KAPPA), axis=1)
    return jnp.where(total > 0.0, top * KAPPA + jnp.log2(total), NEG)


def partial_stats(acc):
    split = acc.reshape(BLK // 8, 8, BLK)
    m = jnp.max(split, axis=0)
    return m, jnp.sum(jnp.exp2((split - m[None]) * KAPPA), axis=0)


def clear(m_ref, s_ref):
    m_ref[...] = jnp.full_like(m_ref, NEG)
    s_ref[...] = jnp.zeros_like(s_ref)


def source_block(x_ref, s):
    return x_ref[s >> 1, :, columns(s & 1)]


def no_tail(index):
    return jnp.zeros((GROUP, BLK), jnp.bfloat16)


def target_by_source(entries, x_ref, yt_ref, hot_ref, tail=no_tail):
    accs = []
    for e in entries:
        source = jnp.minimum(source_of(e), 2 * x_ref.shape[0] - 1)
        parts = [source_block(x_ref, source), hot_ref[e & (GROUP - 1)], tail(source)]
        accs.append(dot(yt_ref[target_of(e) & 31], jnp.concatenate(parts, axis=0)))
    return accs


def source_by_target(entries, pack_ref, xt_ref, hot_ref, tail=no_tail):
    accs = []
    for e in entries:
        source, target = jnp.minimum(source_of(e), xt_ref.shape[0] - 1), target_of(e) & 31
        block = pack_ref[:LAT, columns(target)]
        parts = [block, hot_ref[source & (GROUP - 1)], tail(target)]
        accs.append(dot(xt_ref[source], jnp.concatenate(parts, axis=0)))
    return accs


def plain_sum(acc):
    return jnp.sum(jnp.exp2(acc * KAPPA).reshape(BLK // 8, 8, BLK), axis=0)


def finish_plain(s_ref, bias):
    total = jnp.sum(s_ref[: s_ref.shape[0] - 1], axis=1)
    live = total > 0.0
    return jnp.where(live, jnp.log2(jnp.where(live, total, 1.0)), NEG) - KAPPA * bias


def put_level(level, mass, out_ref):
    out_ref[...] = jnp.broadcast_to((level - mass * (1.0 / LN2))[None], out_ref.shape)


def transposed(block):
    return jnp.concatenate([block, jnp.zeros_like(block)], axis=0).T


def target_side_kernel(pack_ref, yt0_ref, minus_half_ref, hot_ref):
    fill_hot(hot_ref)
    for q in range(yt0_ref.shape[0]):
        block = pack_ref[:LAT, q * BLK : (q + 1) * BLK]
        yt0_ref[q] = transposed(block)
        minus_half_ref[q : q + 1, :] = -0.5 * jnp.sum(
            jnp.square(block.astype(jnp.float32)), axis=0, keepdims=True
        )


def spread_kernel(in_ref, out_ref):
    out_ref[...] = jnp.broadcast_to(in_ref[...][None], out_ref.shape)


def start_copy(from_ref, to_ref, sem):
    copy = pltpu.make_async_copy(from_ref, to_ref, sem)
    copy.start()
    return copy


def first_row_kernel(
    log_ref, tiles_ref, b_ref, hot_ref, x_ref, yt0_ref, out_ref, xt0_ref, list_ref, side_ref, sems, yt_ref, m_ref, s_ref
):
    copy = start_copy(tiles_ref, list_ref, sems.at[0])
    mass = start_copy(log_ref, side_ref.at[0], sems.at[1])
    clear(m_ref, s_ref)
    fill_biased(yt0_ref, b_ref[...], yt_ref)
    for q in range(xt0_ref.shape[0]):
        xt0_ref[q] = transposed(x_ref[q // 2, :, (q % 2) * BLK : (q % 2 + 1) * BLK])
    copy.wait()

    def body(entries):
        stats = [partial_stats(a) for a in target_by_source(entries, x_ref, yt_ref, hot_ref)]
        for e, (m, s) in zip(entries, stats):
            fold_into(source_of(e), m, s, m_ref, s_ref)

    sweep(list_ref, body)
    n = m_ref.shape[0] - 1
    mass.wait()
    put_level(finish(m_ref[:n], s_ref[:n]), side_ref[0], out_ref)


def first_col_kernel(
    log_ref, tiles_ref, hot_ref, xt0_ref, pack_ref, r_ref, out_ref, tail_out_ref, a_ref, list_ref, side_ref, sems, xt_ref, m_ref, s_ref
):
    copy = start_copy(tiles_ref, list_ref, sems.at[0])
    mass = start_copy(log_ref, side_ref.at[0], sems.at[1])
    a = bias_of(join(r_ref[...]))
    side_ref[1] = a
    out_a = start_copy(side_ref.at[1], a_ref, sems.at[2])
    clear(m_ref, s_ref)
    fill_biased(xt0_ref, a, xt_ref)
    fill_tails(a, tail_out_ref)
    copy.wait()

    def body(entries):
        stats = [partial_stats(a) for a in source_by_target(entries, pack_ref, xt_ref, hot_ref)]
        for e, (m, s) in zip(entries, stats):
            fold_into(target_of(e), m, s, m_ref, s_ref)

    sweep(list_ref, body)
    k = m_ref.shape[0] - 1
    mass.wait()
    put_level(finish(m_ref[:k], s_ref[:k]), side_ref[0], out_ref)
    out_a.wait()


def row_kernel(
    log_ref, a_ref, tiles_ref, hot_ref, tail_ref, x_ref, yt0_ref, c_ref, d_ref, out_ref, tail_out_ref, b_ref, list_ref, side_ref, sems, yt_ref, s_ref
):
    copy = start_copy(tiles_ref, list_ref, sems.at[0])
    mass = start_copy(log_ref, side_ref.at[0], sems.at[1])
    in_a = start_copy(a_ref, side_ref.at[2], sems.at[3])
    b = bias_of(join_pair(c_ref[...], d_ref[...]))
    side_ref[1] = b
    out_b = start_copy(side_ref.at[1], b_ref, sems.at[2])
    s_ref[...] = jnp.zeros_like(s_ref)
    fill_biased(yt0_ref, b, yt_ref)
    fill_tails(b, tail_out_ref)
    copy.wait()

    def body(entries):
        accs = target_by_source(entries, x_ref, yt_ref, hot_ref, lambda q: tail_ref[q])
        for e, s in zip(entries, [plain_sum(acc) for acc in accs]):
            s_ref[source_of(e)] += s

    sweep(list_ref, body, PLAIN_TURNS)
    mass.wait()
    in_a.wait()
    put_level(finish_plain(s_ref, side_ref[2]), side_ref[0], out_ref)
    out_b.wait()


def col_kernel(
    log_ref, b_ref, tiles_ref, hot_ref, tail_ref, xt0_ref, pack_ref, r_ref, out_ref, tail_out_ref, a_ref, list_ref, side_ref, sems, xt_ref, s_ref
):
    copy = start_copy(tiles_ref, list_ref, sems.at[0])
    mass = start_copy(log_ref, side_ref.at[0], sems.at[1])
    in_b = start_copy(b_ref, side_ref.at[2], sems.at[3])
    a = bias_of(join(r_ref[...]))
    side_ref[1] = a
    out_a = start_copy(side_ref.at[1], a_ref, sems.at[2])
    s_ref[...] = jnp.zeros_like(s_ref)
    fill_biased(xt0_ref, a, xt_ref)
    fill_tails(a, tail_out_ref)
    copy.wait()

    def body(entries):
        accs = source_by_target(entries, pack_ref, xt_ref, hot_ref, lambda q: tail_ref[q])
        for e, s in zip(entries, [plain_sum(acc) for acc in accs]):
            s_ref[target_of(e)] += s

    sweep(list_ref, body, PLAIN_TURNS)
    mass.wait()
    in_b.wait()
    put_level(finish_plain(s_ref, side_ref[2]), side_ref[0], out_ref)
    out_a.wait()


def project_kernel(
    tiles_ref, hot_ref, tail_ref, x_ref, yt0_ref, pack_ref, c_ref, d_ref, out_ref, b_ref, list_ref, side_ref, sems, yt_ref, w_ref
):
    copy = start_copy(tiles_ref, list_ref, sems.at[0])
    b = bias_of(join_pair(c_ref[...], d_ref[...]))
    side_ref[1] = b
    out_b = start_copy(side_ref.at[1], b_ref, sems.at[2])
    w_ref[...] = jnp.zeros_like(w_ref)
    fill_biased(yt0_ref, b, yt_ref)
    copy.wait()

    def body(entries):
        weighted = []
        accs = target_by_source(entries, x_ref, yt_ref, hot_ref, lambda q: tail_ref[q])
        for e, acc in zip(entries, accs):
            p = jnp.exp2(acc * KAPPA)
            hi = p.astype(jnp.bfloat16)
            low = (p - hi.astype(jnp.float32)).astype(jnp.bfloat16)
            side = pack_ref[LAT:, columns(target_of(e) & 31)]
            both = jnp.concatenate([hi, low], axis=0)
            weighted.append(dot(jnp.concatenate([side, side], axis=1), both)[:8])
        for e, w in zip(entries, weighted):
            w_ref[source_of(e)] += w

    sweep(list_ref, body)
    out_ref[...] = jnp.zeros_like(out_ref)
    for ib in range(2 * x_ref.shape[0]):
        w = w_ref[ib]
        for place, row in enumerate((2, 0, 1)):
            first = 2 * place + ib % 2
            out_ref[ib // 2, first : first + 1, :] = w[row : row + 1]
    out_b.wait()


VMEM = pl.BlockSpec(memory_space=pltpu.VMEM)
HBM = pl.BlockSpec(memory_space=pltpu.HBM)


def call(kernel, outs, scratch, far, near, far_outs=0):
    put = pltpu.with_memory_space_constraint
    return pl.pallas_call(
        kernel,
        out_shape=outs,
        in_specs=[HBM] * len(far) + [VMEM] * len(near),
        out_specs=[VMEM] * (len(outs) - far_outs) + [HBM] * far_outs,
        scratch_shapes=scratch,
        compiler_params=pltpu.CompilerParams(vmem_limit_bytes=16 << 20),
    )(*(put(a, pltpu.HBM) for a in far), *(put(a, pltpu.VMEM) for a in near))


def tile_list(support, chip, core, per_chip, slots):
    rows, per_list = support.shape
    row = jnp.arange(rows, dtype=jnp.int32)[:, None]
    owned = (support // per_chip == chip) & (row // 2 % 2 == core)
    flags = owned.astype(jnp.float32)
    upto = (jnp.arange(per_list)[:, None] <= jnp.arange(per_list)[None, :]).astype(jnp.float32)
    before = (jnp.arange(rows)[None, :] < jnp.arange(rows)[:, None]).astype(jnp.float32)
    within = flags @ upto
    start = before @ within[:, -1:]
    place = jnp.where(owned, (within + start).astype(jnp.int32) - 1, -1)
    code = (row // 4 * 2 + row % 2) * 64 + support % per_chip - PAD
    slot = jnp.arange(slots + BLK, dtype=jnp.int32).reshape(-1, BLK)
    place, code = place[:, :, None, None], code[:, :, None, None]
    last = jnp.where((slot >= slots) & (place >= 0), 1, 0)
    listed = jnp.where(place == slot, code, last)
    return jnp.sum(listed, axis=(0, 1), dtype=jnp.int32), within


def on_device(
    source_latent, target_latent, log_source_mass, log_target_mass, target_coords, support
):
    rows, cols = lax.axis_size("row"), lax.axis_size("col")
    here = lax.axis_index("col")
    chip, core = here // 2, here % 2
    chips = cols // 2
    mine = support.shape[0] // cols
    own_k = target_latent.shape[1] // BLK
    n, k = chips * mine, 2 * own_k
    bf16, f32 = jnp.bfloat16, jnp.float32
    by_chip = chip_groups(cols)

    def of_core(a):
        split = a.reshape((chips, 2, mine) + a.shape[1:])
        split = jnp.where(core == 0, split[:, 0], split[:, 1])
        return split.reshape((n,) + a.shape[1:])

    spread = pl.pallas_call(
        spread_kernel,
        out_shape=jax.ShapeDtypeStruct((chips,) + source_latent.shape, bf16),
        in_specs=[VMEM],
        out_specs=VMEM,
    )(source_latent)
    spread, support = lax.optimization_barrier((spread, support))
    x = exchange(spread, "col", by_chip)
    tiles, early = tile_list(support, chip, core, k, 12 * mine * chips)
    early, target_latent, target_coords, log_target_mass = lax.optimization_barrier(
        (early, target_latent, target_coords, log_target_mass)
    )

    def pair(a):
        other = swap_cores(a, cols)
        return jnp.concatenate(
            [jnp.where(core == 0, a, other), jnp.where(core == 0, other, a)], axis=1
        )

    width = 2 * target_latent.shape[1]
    targets = pair(target_latent)
    coords, target_log = pair(target_coords), pair(log_target_mass[None])
    pack = jnp.concatenate(
        [targets, coords, jnp.ones((1, width), bf16), jnp.zeros((PACK - LAT - 3, width), bf16)],
        axis=0,
    )
    common = [
        pltpu.SMEM(tiles.shape, jnp.int32),
        pltpu.VMEM((3, n, BLK), f32),
        pltpu.SemaphoreType.DMA((4,)),
        pltpu.VMEM((n, BLK, BLK), bf16),
    ]
    sums = pltpu.VMEM((n + 1, 8, BLK), f32)
    first_scratch = common + [sums, sums]
    scratch = common + [sums]

    target_log = target_log.astype(f32).reshape(k, BLK)
    source_log = of_core(log_source_mass.reshape(-1, BLK))
    tiles, source_log, target_log = lax.optimization_barrier((tiles, source_log, target_log))

    turned = pltpu.VMEM((n, BLK, BLK), bf16)
    hot_shape = pltpu.VMEM((GROUP, 3 * GROUP, BLK), bf16)
    yt0, minus_half, hot = call(
        target_side_kernel, [turned, pltpu.VMEM((k, BLK), f32), hot_shape], [], [], [pack]
    )
    tail_shape = pltpu.VMEM((n, GROUP, BLK), bf16)
    small = pltpu.HBM((n, BLK), f32)
    to_chips = jax.ShapeDtypeStruct((chips, n, BLK), f32)
    to_rows = jax.ShapeDtypeStruct((rows, k, BLK), f32)
    to_owners = jax.ShapeDtypeStruct((chips, 8, BLK), f32)
    by_sources, by_targets = [source_log], [target_log]

    r, xt0 = call(
        first_row_kernel,
        [to_chips, turned],
        first_scratch,
        by_sources,
        [tiles, minus_half, hot, x, yt0],
    )
    r = exchange(r, "col", by_chip)
    c, tail, a = call(
        first_col_kernel,
        [to_rows, tail_shape, small],
        first_scratch,
        by_targets,
        [tiles, hot, xt0, pack, r],
        1,
    )
    c = exchange(c, "row")
    d = swap_cores(c, cols)
    r, tail, b = call(
        row_kernel,
        [to_chips, tail_shape, small],
        scratch,
        by_sources + [a],
        [tiles, hot, tail, x, yt0, c, d],
        1,
    )
    r = exchange(r, "col", by_chip)
    c, tail, a = call(
        col_kernel,
        [to_rows, tail_shape, small],
        scratch,
        by_targets + [b],
        [tiles, hot, tail, xt0, pack, r],
        1,
    )
    c = exchange(c, "row")
    d = swap_cores(c, cols)
    part, b = call(
        project_kernel,
        [to_owners, small],
        scratch,
        [],
        [tiles, hot, tail, x, yt0, pack, c, d],
        1,
    )
    part, a, b, source_latent = lax.optimization_barrier((part, a, b, source_latent))
    part = jnp.sum(exchange(part, "col", by_chip), axis=0)
    mapped = part[mine : 3 * mine].reshape(2, mine, BLK) / part[:mine]
    mapped = mapped.reshape(2, mine * BLK)

    own_a = lax.dynamic_slice_in_dim(a, chip * mine, mine).reshape(-1)
    x_half = 0.5 * jnp.sum(jnp.square(source_latent.astype(f32)), axis=0)
    out_source = (own_a + x_half) / 32.0
    out_target = lax.dynamic_slice_in_dim((b - minus_half) / 32.0, core * own_k, own_k).reshape(-1)
    return out_source, out_target, mapped


def solution(mesh):
    in_specs = (
        P(None, ("row", "col")),
        P(None, "col"),
        P("row"),
        P("col"),
        P(None, "col"),
        P("row", None),
    )
    out_specs = (P(("row", "col")), P("col"), P(None, ("row", "col")))
    return jax.shard_map(
        on_device, mesh=mesh, in_specs=in_specs, out_specs=out_specs, check_vma=False
    )
```

```python
import functools

import jax
import jax.numpy as jnp
from jax import lax
from jax.experimental import pallas as pl
from jax.experimental.pallas import tpu as pltpu
from jax.sharding import PartitionSpec as P

LAT = 64
BLK = 128
NEG = -1e30
LN2 = 0.6931471805599453
KAPPA = 0.3125 / LN2
PLAIN_TURNS = (128, 64, 32, 16)
TURNS = (64, 16)
PACK = 80
GROUP = 16
PAD = 32 * 64 + 32


def chip_groups(cols):
    return [[c for c in range(cols) if c % 2 == core] for core in range(2)]


def swap_cores(x, cols):
    return lax.ppermute(x, "col", [(i, i ^ 1) for i in range(cols)])


def exchange(x, axis, groups=None):
    return lax.all_to_all(x, axis, 0, 0, axis_index_groups=groups)


def join(parts):
    top = jnp.max(parts, axis=0)
    return top + jnp.log2(jnp.sum(jnp.exp2(parts - top[None]), axis=0))


def join_pair(a, b):
    top = jnp.maximum(jnp.max(a, axis=0), jnp.max(b, axis=0))
    total = jnp.sum(jnp.exp2(a - top[None]), axis=0) + jnp.sum(jnp.exp2(b - top[None]), axis=0)
    return top + jnp.log2(total)


def bias_of(level):
    return -3.2 * LN2 * level


def pieces(a):
    hi = a.astype(jnp.bfloat16)
    rest = a - hi.astype(jnp.float32)
    mid = rest.astype(jnp.bfloat16)
    low = (rest - mid.astype(jnp.float32)).astype(jnp.bfloat16)
    return hi, mid, low


def fill_hot(hot_ref):
    row = lax.broadcasted_iota(jnp.int32, hot_ref.shape[1:], 0)
    for q in range(GROUP):
        hot_ref[q] = jnp.where((row & (GROUP - 1)) == q, 1.0, 0.0).astype(jnp.bfloat16)


def fill_biased(plain_ref, bias, full_ref):
    for first in range(0, plain_ref.shape[0], GROUP):
        hi, mid, low = pieces(bias[first : first + GROUP])
        blank = jnp.zeros((LAT, BLK), jnp.bfloat16)
        side = jnp.concatenate([blank, hi, mid, low, jnp.ones_like(hi)], axis=0).T
        for block in range(first, first + GROUP):
            full_ref[block] = plain_ref[block] + side


def fill_tails(bias, tail_ref):
    row = lax.broadcasted_iota(jnp.int32, (GROUP, BLK), 0)
    hi, mid, low = (p.astype(jnp.float32) for p in pieces(bias))
    for block in range(bias.shape[0]):
        one = slice(block, block + 1)
        rows = jnp.where(row == 1, mid[one], jnp.where(row == 2, low[one], 0.0))
        tail_ref[block] = jnp.where(row == 0, hi[one], rows).astype(jnp.bfloat16)


def columns(jb):
    return pl.ds(pl.multiple_of(jb * BLK, BLK), BLK)


def dot(lhs, rhs):
    return jnp.dot(lhs, rhs, preferred_element_type=jnp.float32)


def sweep(list_ref, body, sizes=TURNS):
    count = list_ref[list_ref.shape[0] - 1, 0]
    done = 0
    for size in sizes:
        left = jnp.maximum(count - done, 0)
        turns = (left + (size // 4 if size > sizes[-1] else size) - 1) // size

        def turn(g, c, size=size, done=done):
            first = done + g * size
            row, start = first // BLK, first % BLK
            body([list_ref[row, start + u] + PAD for u in range(size)])
            return c

        lax.fori_loop(0, turns, turn, 0)
        done = done + turns * size


def source_of(e):
    return e >> 6


def target_of(e):
    return e & 63


def fold_into(index, m, s, m_ref, s_ref):
    old = m_ref[index]
    new = jnp.maximum(old, m)
    s_ref[index] = s_ref[index] * jnp.exp2((old - new) * KAPPA) + s * jnp.exp2((m - new) * KAPPA)
    m_ref[index] = new


def finish(m, s):
    top = jnp.max(m, axis=1)
    total = jnp.sum(s * jnp.exp2((m - top[:, None, :]) * KAPPA), axis=1)
    return jnp.where(total > 0.0, top * KAPPA + jnp.log2(total), NEG)


def partial_stats(acc):
    split = acc.reshape(BLK // 8, 8, BLK)
    m = jnp.max(split, axis=0)
    return m, jnp.sum(jnp.exp2((split - m[None]) * KAPPA), axis=0)


def clear(m_ref, s_ref):
    m_ref[...] = jnp.full_like(m_ref, NEG)
    s_ref[...] = jnp.zeros_like(s_ref)


def source_block(x_ref, s):
    return x_ref[s >> 1, :, columns(s & 1)]


def no_tail(index):
    return jnp.zeros((GROUP, BLK), jnp.bfloat16)


def target_by_source(entries, x_ref, yt_ref, hot_ref, tail=no_tail):
    accs = []
    for e in entries:
        source = jnp.minimum(source_of(e), 2 * x_ref.shape[0] - 1)
        parts = [source_block(x_ref, source), hot_ref[e & (GROUP - 1)], tail(source)]
        accs.append(dot(yt_ref[target_of(e) & 31], jnp.concatenate(parts, axis=0)))
    return accs


def source_by_target(entries, pack_ref, xt_ref, hot_ref, tail=no_tail):
    accs = []
    for e in entries:
        source, target = jnp.minimum(source_of(e), xt_ref.shape[0] - 1), target_of(e) & 31
        block = pack_ref[:LAT, columns(target)]
        parts = [block, hot_ref[source & (GROUP - 1)], tail(target)]
        accs.append(dot(xt_ref[source], jnp.concatenate(parts, axis=0)))
    return accs


def plain_sum(acc):
    return jnp.sum(jnp.exp2(acc * KAPPA).reshape(BLK // 8, 8, BLK), axis=0)


def finish_plain(s_ref, bias):
    total = jnp.sum(s_ref[: s_ref.shape[0] - 1], axis=1)
    live = total > 0.0
    return jnp.where(live, jnp.log2(jnp.where(live, total, 1.0)), NEG) - KAPPA * bias


def put_level(level, mass, out_ref):
    out_ref[...] = jnp.broadcast_to((level - mass * (1.0 / LN2))[None], out_ref.shape)


def transposed(block):
    return jnp.concatenate([block, jnp.zeros_like(block)], axis=0).T


def target_side_kernel(pack_ref, yt0_ref, first_ref, hot_ref, minus_half_ref):
    fill_hot(hot_ref)
    for q in range(yt0_ref.shape[0]):
        block = pack_ref[:LAT, q * BLK : (q + 1) * BLK]
        yt0_ref[q] = transposed(block)
        minus_half_ref[q : q + 1, :] = -0.5 * jnp.sum(
            jnp.square(block.astype(jnp.float32)), axis=0, keepdims=True
        )
    fill_biased(yt0_ref, minus_half_ref[...], first_ref)


def spread_kernel(in_ref, out_ref):
    out_ref[...] = jnp.broadcast_to(in_ref[...][None], out_ref.shape)


def start_copy(from_ref, to_ref, sem):
    copy = pltpu.make_async_copy(from_ref, to_ref, sem)
    copy.start()
    return copy


def first_row_kernel(
    log_ref, tiles_ref, hot_ref, x_ref, yt_ref, out_ref, xt0_ref, list_ref, side_ref, sems, full_ref, m_ref, s_ref
):
    copy = start_copy(tiles_ref, list_ref, sems.at[0])
    mass = start_copy(log_ref, side_ref.at[0], sems.at[1])
    clear(m_ref, s_ref)
    for q in range(xt0_ref.shape[0]):
        xt0_ref[q] = transposed(x_ref[q // 2, :, (q % 2) * BLK : (q % 2 + 1) * BLK])
    copy.wait()

    def body(entries):
        stats = [partial_stats(a) for a in target_by_source(entries, x_ref, yt_ref, hot_ref)]
        for e, (m, s) in zip(entries, stats):
            fold_into(source_of(e), m, s, m_ref, s_ref)

    sweep(list_ref, body)
    n = m_ref.shape[0] - 1
    mass.wait()
    put_level(finish(m_ref[:n], s_ref[:n]), side_ref[0], out_ref)


def first_col_kernel(
    log_ref, tiles_ref, hot_ref, xt0_ref, pack_ref, r_ref, out_ref, tail_out_ref, a_ref, list_ref, side_ref, sems, xt_ref, m_ref, s_ref
):
    copy = start_copy(tiles_ref, list_ref, sems.at[0])
    mass = start_copy(log_ref, side_ref.at[0], sems.at[1])
    a = bias_of(join(r_ref[...]))
    side_ref[1] = a
    out_a = start_copy(side_ref.at[1], a_ref, sems.at[2])
    clear(m_ref, s_ref)
    fill_biased(xt0_ref, a, xt_ref)
    fill_tails(a, tail_out_ref)
    copy.wait()

    def body(entries):
        stats = [partial_stats(a) for a in source_by_target(entries, pack_ref, xt_ref, hot_ref)]
        for e, (m, s) in zip(entries, stats):
            fold_into(target_of(e), m, s, m_ref, s_ref)

    sweep(list_ref, body)
    k = m_ref.shape[0] - 1
    mass.wait()
    put_level(finish(m_ref[:k], s_ref[:k]), side_ref[0], out_ref)
    out_a.wait()


def row_kernel(
    log_ref, a_ref, tiles_ref, hot_ref, tail_ref, x_ref, yt0_ref, c_ref, d_ref, out_ref, tail_out_ref, b_ref, list_ref, side_ref, sems, yt_ref, s_ref
):
    copy = start_copy(tiles_ref, list_ref, sems.at[0])
    mass = start_copy(log_ref, side_ref.at[0], sems.at[1])
    in_a = start_copy(a_ref, side_ref.at[2], sems.at[3])
    b = bias_of(join_pair(c_ref[...], d_ref[...]))
    side_ref[1] = b
    out_b = start_copy(side_ref.at[1], b_ref, sems.at[2])
    s_ref[...] = jnp.zeros_like(s_ref)
    fill_biased(yt0_ref, b, yt_ref)
    fill_tails(b, tail_out_ref)
    copy.wait()

    def body(entries):
        accs = target_by_source(entries, x_ref, yt_ref, hot_ref, lambda q: tail_ref[q])
        for e, s in zip(entries, [plain_sum(acc) for acc in accs]):
            s_ref[source_of(e)] += s

    sweep(list_ref, body, PLAIN_TURNS)
    mass.wait()
    in_a.wait()
    put_level(finish_plain(s_ref, side_ref[2]), side_ref[0], out_ref)
    out_b.wait()


def col_kernel(
    log_ref, b_ref, half_ref, tiles_ref, hot_ref, tail_ref, xt0_ref, pack_ref, r_ref, out_ref, tail_out_ref, source_ref, list_ref, side_ref, sems, xt_ref, s_ref
):
    copy = start_copy(tiles_ref, list_ref, sems.at[0])
    mass = start_copy(log_ref, side_ref.at[0], sems.at[1])
    in_b = start_copy(b_ref, side_ref.at[2], sems.at[3])
    mine = half_ref.shape[0]
    half = start_copy(half_ref, side_ref.at[3, pl.ds(0, mine)], sems.at[4])
    a = bias_of(join(r_ref[...]))
    side_ref[1] = a
    s_ref[...] = jnp.zeros_like(s_ref)
    fill_biased(xt0_ref, a, xt_ref)
    fill_tails(a, tail_out_ref)
    copy.wait()
    half.wait()
    own = side_ref[1, pl.ds(lax.axis_index("col") // 2 * mine, mine), :]
    side_ref[3, 8 : 8 + mine, :] = (own + side_ref[3, :mine, :]) * (1.0 / 32)
    potential = start_copy(side_ref.at[3, pl.ds(8, mine)], source_ref, sems.at[2])

    def body(entries):
        accs = source_by_target(entries, pack_ref, xt_ref, hot_ref, lambda q: tail_ref[q])
        for e, s in zip(entries, [plain_sum(acc) for acc in accs]):
            s_ref[target_of(e)] += s

    sweep(list_ref, body, PLAIN_TURNS)
    mass.wait()
    in_b.wait()
    put_level(finish_plain(s_ref, side_ref[2]), side_ref[0], out_ref)
    potential.wait()


def project_kernel(
    half_ref, tiles_ref, hot_ref, tail_ref, x_ref, yt0_ref, pack_ref, c_ref, d_ref, out_ref, target_ref, list_ref, side_ref, sems, yt_ref, w_ref
):
    copy = start_copy(tiles_ref, list_ref, sems.at[0])
    half = start_copy(half_ref, side_ref.at[2], sems.at[1])
    b = bias_of(join_pair(c_ref[...], d_ref[...]))
    w_ref[...] = jnp.zeros_like(w_ref)
    fill_biased(yt0_ref, b, yt_ref)
    copy.wait()
    half.wait()
    side_ref[1] = (b - side_ref[2]) * (1.0 / 32)
    own_k = target_ref.shape[0]
    first = pl.multiple_of(lax.axis_index("col") % 2 * own_k, own_k)
    potential = start_copy(side_ref.at[1, pl.ds(first, own_k)], target_ref, sems.at[2])

    def body(entries):
        weighted = []
        accs = target_by_source(entries, x_ref, yt_ref, hot_ref, lambda q: tail_ref[q])
        for e, acc in zip(entries, accs):
            p = jnp.exp2(acc * KAPPA)
            hi = p.astype(jnp.bfloat16)
            low = (p - hi.astype(jnp.float32)).astype(jnp.bfloat16)
            side = pack_ref[LAT:, columns(target_of(e) & 31)]
            both = jnp.concatenate([hi, low], axis=0)
            weighted.append(dot(jnp.concatenate([side, side], axis=1), both)[:8])
        for e, w in zip(entries, weighted):
            w_ref[source_of(e)] += w

    sweep(list_ref, body)
    out_ref[...] = jnp.zeros_like(out_ref)
    for ib in range(2 * x_ref.shape[0]):
        w = w_ref[ib]
        for place, row in enumerate((2, 0, 1)):
            first = 2 * place + ib % 2
            out_ref[ib // 2, first : first + 1, :] = w[row : row + 1]
    potential.wait()


VMEM = pl.BlockSpec(memory_space=pltpu.VMEM)
HBM = pl.BlockSpec(memory_space=pltpu.HBM)


def call(kernel, outs, scratch, far, near, far_outs=0):
    put = pltpu.with_memory_space_constraint
    return pl.pallas_call(
        kernel,
        out_shape=outs,
        in_specs=[HBM] * len(far) + [VMEM] * len(near),
        out_specs=[VMEM] * (len(outs) - far_outs) + [HBM] * far_outs,
        scratch_shapes=scratch,
        compiler_params=pltpu.CompilerParams(vmem_limit_bytes=16 << 20),
    )(*(put(a, pltpu.HBM) for a in far), *(put(a, pltpu.VMEM) for a in near))


def tile_list(support, chip, core, per_chip, slots):
    rows, per_list = support.shape
    row = jnp.arange(rows, dtype=jnp.int32)[:, None]
    owned = (support // per_chip == chip) & (row // 2 % 2 == core)
    flags = owned.astype(jnp.float32)
    upto = (jnp.arange(per_list)[:, None] <= jnp.arange(per_list)[None, :]).astype(jnp.float32)
    before = (jnp.arange(rows)[None, :] < jnp.arange(rows)[:, None]).astype(jnp.float32)
    within = flags @ upto
    start = before @ within[:, -1:]
    place = jnp.where(owned, (within + start).astype(jnp.int32) - 1, -1)
    code = (row // 4 * 2 + row % 2) * 64 + support % per_chip - PAD
    slot = jnp.arange(slots + BLK, dtype=jnp.int32).reshape(-1, BLK)
    place, code = place[:, :, None, None], code[:, :, None, None]
    last = jnp.where((slot >= slots) & (place >= 0), 1, 0)
    listed = jnp.where(place == slot, code, last)
    return jnp.sum(listed, axis=(0, 1), dtype=jnp.int32), within


def on_device(
    source_latent, target_latent, log_source_mass, log_target_mass, target_coords, support
):
    rows, cols = lax.axis_size("row"), lax.axis_size("col")
    here = lax.axis_index("col")
    chip, core = here // 2, here % 2
    chips = cols // 2
    mine = support.shape[0] // cols
    own_k = target_latent.shape[1] // BLK
    n, k = chips * mine, 2 * own_k
    bf16, f32 = jnp.bfloat16, jnp.float32
    by_chip = chip_groups(cols)

    def of_core(a):
        split = a.reshape((chips, 2, mine) + a.shape[1:])
        split = jnp.where(core == 0, split[:, 0], split[:, 1])
        return split.reshape((n,) + a.shape[1:])

    spread = pl.pallas_call(
        spread_kernel,
        out_shape=jax.ShapeDtypeStruct((chips,) + source_latent.shape, bf16),
        in_specs=[VMEM],
        out_specs=VMEM,
    )(source_latent)
    spread, support = lax.optimization_barrier((spread, support))
    x = exchange(spread, "col", by_chip)
    tiles, early = tile_list(support, chip, core, k, 12 * mine * chips)
    early, target_latent, target_coords, log_target_mass, source_latent = (
        lax.optimization_barrier(
            (early, target_latent, target_coords, log_target_mass, source_latent)
        )
    )

    def pair(a):
        other = swap_cores(a, cols)
        return jnp.concatenate(
            [jnp.where(core == 0, a, other), jnp.where(core == 0, other, a)], axis=1
        )

    width = 2 * target_latent.shape[1]
    targets = pair(target_latent)
    coords, target_log = pair(target_coords), pair(log_target_mass[None])
    pack = jnp.concatenate(
        [targets, coords, jnp.ones((1, width), bf16), jnp.zeros((PACK - LAT - 3, width), bf16)],
        axis=0,
    )
    common = [
        pltpu.SMEM(tiles.shape, jnp.int32),
        pltpu.VMEM((4, n, BLK), f32),
        pltpu.SemaphoreType.DMA((5,)),
        pltpu.VMEM((n, BLK, BLK), bf16),
    ]
    sums = pltpu.VMEM((n + 1, 8, BLK), f32)
    first_scratch = common + [sums, sums]
    scratch = common + [sums]

    target_log = target_log.astype(f32).reshape(k, BLK)
    source_log = of_core(log_source_mass.reshape(-1, BLK))
    x_half = 0.5 * jnp.sum(jnp.square(source_latent.astype(f32)), axis=0).reshape(mine, BLK)
    tiles, source_log, target_log, x_half = lax.optimization_barrier(
        (tiles, source_log, target_log, x_half)
    )

    turned = pltpu.VMEM((n, BLK, BLK), bf16)
    hot_shape = pltpu.VMEM((GROUP, 3 * GROUP, BLK), bf16)
    small = pltpu.HBM((n, BLK), f32)
    yt0, yt_first, hot, minus_half = call(
        target_side_kernel,
        [turned, turned, hot_shape, pltpu.VMEM((k, BLK), f32)],
        [],
        [],
        [pack],
    )
    tail_shape = pltpu.VMEM((n, GROUP, BLK), bf16)
    to_chips = jax.ShapeDtypeStruct((chips, n, BLK), f32)
    to_rows = jax.ShapeDtypeStruct((rows, k, BLK), f32)
    to_owners = jax.ShapeDtypeStruct((chips, 8, BLK), f32)
    by_sources, by_targets = [source_log], [target_log]

    r, xt0 = call(
        first_row_kernel,
        [to_chips, turned],
        first_scratch,
        by_sources,
        [tiles, hot, x, yt_first],
    )
    r = exchange(r, "col", by_chip)
    c, tail, a = call(
        first_col_kernel,
        [to_rows, tail_shape, small],
        first_scratch,
        by_targets,
        [tiles, hot, xt0, pack, r],
        1,
    )
    c = exchange(c, "row")
    d = swap_cores(c, cols)
    r, tail, b = call(
        row_kernel,
        [to_chips, tail_shape, small],
        scratch,
        by_sources + [a],
        [tiles, hot, tail, x, yt0, c, d],
        1,
    )
    r = exchange(r, "col", by_chip)
    c, tail, out_source = call(
        col_kernel,
        [to_rows, tail_shape, pltpu.HBM((mine, BLK), f32)],
        scratch,
        by_targets + [b, x_half],
        [tiles, hot, tail, xt0, pack, r],
        1,
    )
    c = exchange(c, "row")
    d = swap_cores(c, cols)
    part, out_target = call(
        project_kernel,
        [to_owners, pltpu.HBM((own_k, BLK), f32)],
        scratch,
        [minus_half],
        [tiles, hot, tail, x, yt0, pack, c, d],
        1,
    )
    part = jnp.sum(exchange(part, "col", by_chip), axis=0)
    mapped = part[mine : 3 * mine].reshape(2, mine, BLK) / part[:mine]
    mapped = mapped.reshape(2, mine * BLK)
    return out_source.reshape(-1), out_target.reshape(-1), mapped


def solution(mesh):
    in_specs = (
        P(None, ("row", "col")),
        P(None, "col"),
        P("row"),
        P("col"),
        P(None, "col"),
        P("row", None),
    )
    out_specs = (P(("row", "col")), P("col"), P(None, ("row", "col")))
    return jax.shard_map(
        on_device, mesh=mesh, in_specs=in_specs, out_specs=out_specs, check_vma=False
    )
```
